32 devices in a mesh: ctx: 4 (over y, core), section: 2 (over x), tp: 4 (over z).
Axes of the slice: x: 2, y: 2, z: 4, core: 2. Of those that a mesh axis runs over, the one named last changes fastest.
Arguments:
- row_offsets: int32 [2], P('section'), may hold values from 1408 to 2048
- queries: bfloat16 [2, 512, 4096], P('section', 'ctx', 'tp'), may hold values from -8 to 8
- cache_keys: bfloat16 [2, 2560, 1024], P('section', 'ctx', 'tp'), may hold values from -4 to 4
- cache_values: bfloat16 [2, 2560, 1024], P('section', 'ctx', 'tp'), may hold values from -6 to 6
- residual: bfloat16 [2, 512, 5120], P('section', 'ctx', 'tp'), may hold values from -6 to 6
- out_weight: bfloat16 [2, 4096, 5120], P('section', 'tp'), may hold values from -0.09375 to 0.09375
Outputs:
- next_inputs: bfloat16 [2, 512, 5120], P('section', 'ctx', 'tp')
The draws below stay inside these ranges and needn't reach their ends.
All inputs are finite; a program needn't handle non-finite values.
Results may differ from the reference program's by a relative error of at most 0.0085.
Values may be sent and summed in bfloat16 or wider, within the bound.
No kernel may reach another device: no remote copies, remote signals or barrier semaphores. Data moves between devices by JAX's collectives and lax.ppermute only.
A program may use at most 64 MiB of HBM per device.

```python
import jax
import jax.numpy as jnp
from jax import lax

D = 5120
H = 32
KVH = 8
HD = 128
G = 4
S_LOC = 640
MICRO = 2
ROWS = 512
CACHE = 2560
N_TP = 4


def draw_queries(key, part):
    base_key = jax.random.fold_in(key, 11)
    sample = 2.0 * jax.random.normal(jax.random.fold_in(base_key, 3), (MICRO, ROWS, H * HD), jnp.float32)
    sample = jnp.clip(sample, -8.0, 8.0)
    return sample.astype(jnp.bfloat16)


def draw_cache_keys(key, part):
    base_key = jax.random.fold_in(key, 23)
    sample = jax.random.normal(jax.random.fold_in(base_key, 3), (MICRO, CACHE, KVH * HD), jnp.float32)
    sample = jnp.clip(sample, -4.0, 4.0)
    return sample.astype(jnp.bfloat16)


def block_scale(rng, shape, shards, least, top_value):
    gain, own = 1.0, jax.random.fold_in(rng, 6)
    for dim, parts in shards:
        draws = jnp.exp(jax.random.uniform(jax.random.fold_in(own, dim), (parts,), jnp.float32, least / len(shards), top_value / len(shards)))
        gain = gain * jnp.repeat(draws, shape[dim] // parts).reshape([-1 if axis == dim else 1 for axis in range(len(shape))])
    return gain


def bell_draw(key, dims, deviation, limit, pieces=(), kind=jnp.bfloat16):
    values = jax.random.normal(key, dims, jnp.float32) * deviation
    if len(pieces) > 0:
        values = block_scale(key, dims, pieces, -0.22, 0.18) * values
    return jnp.clip(values, min=-limit, max=limit).astype(kind)


def setup_inputs(seed: int = 0) -> dict:
    keys = jax.random.split(jax.random.key(seed), 7)
    row_offsets = jax.random.randint(keys[0], (MICRO,), CACHE - ROWS - S_LOC, CACHE - ROWS + 1).astype(jnp.int32)
    queries = draw_queries(jax.random.fold_in(keys[6], 71), 0)
    cache_keys = draw_cache_keys(jax.random.fold_in(keys[6], 71), 0)
    cache_values = bell_draw(keys[3], (MICRO, CACHE, KVH * HD), 1.0, 6.0, ((0, 2), (1, 4), (2, 4)))
    residual = bell_draw(keys[4], (MICRO, ROWS, D), 1.0, 6.0, ((0, 2), (1, 4), (2, 4)))
    out_weight = bell_draw(keys[5], (MICRO, H * HD, D), (H * HD) ** -0.5, 0.09375, ((0, 2), (1, 4)))
    return dict(row_offsets=row_offsets, queries=queries, cache_keys=cache_keys, cache_values=cache_values, residual=residual, out_weight=out_weight)


def attend_section(offset, query_rows, key_rows, value_rows):
    query_heads = query_rows.reshape(ROWS, KVH, G, HD).transpose(1, 0, 2, 3)
    key_heads = key_rows.reshape(CACHE, KVH, HD).transpose(1, 0, 2)
    value_heads = value_rows.reshape(CACHE, KVH, HD).transpose(1, 0, 2)
    query_pos = offset + jnp.arange(ROWS, dtype=jnp.int32)
    key_pos = jnp.arange(CACHE, dtype=jnp.int32)
    visible = key_pos[None, :] <= query_pos[:, None]

    def one_group(operands):
        query_group, key_group, value_group = operands
        scores = jnp.einsum("qgd,sd->gqs", query_group.astype(jnp.float32), key_group.astype(jnp.float32)) * (HD ** -0.5)
        scores = jnp.where(visible[None], scores, -jnp.inf)
        row_max = jnp.max(scores, axis=-1, keepdims=True)
        weights = jnp.where(visible[None], jnp.exp(scores - row_max), 0.0)
        row_sum = jnp.sum(weights, axis=-1, keepdims=True)
        rounded = lax.optimization_barrier(weights.astype(jnp.bfloat16)).astype(jnp.float32)
        mixed = jnp.einsum("gqs,sd->gqd", rounded, value_group.astype(jnp.float32))
        return mixed / row_sum

    result = lax.map(one_group, (query_heads, key_heads, value_heads))
    return result.transpose(2, 0, 1, 3).reshape(ROWS, H * HD).astype(jnp.bfloat16)


def reference(row_offsets, queries, cache_keys, cache_values, residual, out_weight):
    group_width = H * HD // N_TP
    outputs = []
    for section_index in range(MICRO):
        attended = attend_section(row_offsets[section_index], queries[section_index], cache_keys[section_index], cache_values[section_index])
        projected = jnp.zeros((ROWS, D), jnp.float32)
        for group_index in range(N_TP):
            lower = group_index * group_width
            upper = lower + group_width
            partial_term = jnp.dot(attended[:, lower:upper], out_weight[section_index, lower:upper], preferred_element_type=jnp.float32)
            projected = projected + lax.optimization_barrier(partial_term.astype(jnp.bfloat16)).astype(jnp.float32)
        outputs.append((residual[section_index].astype(jnp.float32) + projected).astype(jnp.bfloat16))
    return jnp.roll(jnp.stack(outputs), 1, axis=0)
```

```python
import functools
import math

import jax
import jax.numpy as jnp
from jax import lax
from jax.experimental import pallas as pl
from jax.experimental.pallas import tpu as pltpu
from jax.sharding import PartitionSpec as P

HD = 128
G = 4
LANES = 128
NEG_FILL = -1e30
MAX_FLOOR = -1e29
EXP_SCALE = HD ** (-0.5) * math.log2(math.e)
MIB = 1 << 20

WHOLE = pl.BlockSpec(memory_space=pltpu.VMEM)
SCALARS = pl.BlockSpec(memory_space=pltpu.SMEM)


def exchange(block, axis, mask):
    route = [(i, i ^ mask) for i in range(lax.axis_size(axis))]
    return lax.ppermute(block, axis, route)


def from_behind(block, axis, distance):
    devices = range(lax.axis_size(axis))
    route = [((i - distance) % len(devices), i) for i in devices]
    return lax.ppermute(block, axis, route)


def in_vmem(array):
    return pltpu.with_memory_space_constraint(array, pltpu.VMEM)


def local_call(body, outs, limit, flops, scratch=()):
    return pl.pallas_call(
        body,
        out_shape=[pltpu.VMEM(shape, dtype) for shape, dtype in outs],
        out_specs=[WHOLE] * len(outs),
        scratch_shapes=list(scratch),
        compiler_params=pltpu.CompilerParams(vmem_limit_bytes=limit),
        cost_estimate=pl.CostEstimate(flops=flops, bytes_accessed=0, transcendentals=0),
    )


def stacked_query(q_ref, kv_head):
    heads = range(kv_head * G, (kv_head + 1) * G)
    return jnp.concatenate([q_ref[0, :, h * HD : (h + 1) * HD] for h in heads], axis=0)


def masked_scores(query, key_ref, kv_head, bound):
    keys = key_ref[0, :, kv_head * HD : (kv_head + 1) * HD]
    scores = lax.dot_general(query, keys, (((1,), (1,)), ((), ())), preferred_element_type=jnp.float32)
    rows = query.shape[0] // G
    ahead = lax.broadcasted_iota(jnp.int32, scores.shape, 1) - lax.broadcasted_iota(jnp.int32, scores.shape, 0) % rows
    return jnp.where(ahead <= bound, scores, NEG_FILL)


def early_kernel(masks, offset_ref, q_ref, *refs):
    count = len(masks)
    key_refs, value_refs = refs[:count], refs[count : 2 * count]
    max_ref, sum_ref, acc_ref = refs[2 * count :]
    own = lax.axis_index("ctx")
    rows, length = q_ref.shape[1], key_refs[0].shape[1]
    first_row = offset_ref[0] + own * rows
    for kv_head in range(key_refs[0].shape[2] // HD):
        columns = slice(kv_head * HD, (kv_head + 1) * HD)
        query = stacked_query(q_ref, kv_head)
        parts = [
            masked_scores(query, ref, kv_head, first_row - (own ^ mask) * length) for ref, mask in zip(key_refs, masks)
        ]
        top = functools.reduce(jnp.maximum, [jnp.max(part, axis=1, keepdims=True) for part in parts])
        top = jnp.maximum(top, MAX_FLOOR)
        weights = [jnp.exp2((part - top) * EXP_SCALE) for part in parts]
        total = sum(jnp.sum(part, axis=1, keepdims=True) for part in weights)
        mixed = sum(
            jnp.dot(part.astype(jnp.bfloat16), ref[0, :, columns], preferred_element_type=jnp.float32)
            for part, ref in zip(weights, value_refs)
        )
        max_ref[kv_head] = jnp.broadcast_to(top, max_ref.shape[1:])
        sum_ref[kv_head] = jnp.broadcast_to(total, sum_ref.shape[1:])
        acc_ref[kv_head] = mixed


def late_kernel(masks, offset_ref, q_ref, max_ref, sum_ref, acc_ref, *refs):
    count = len(masks)
    key_refs = refs[:count]
    total_ref, scaled_ref = refs[count : count + 2]
    weight_refs = refs[count + 2 :]
    own = lax.axis_index("ctx")
    rows, length = q_ref.shape[1], key_refs[0].shape[1]
    first_row = offset_ref[0] + own * rows
    for kv_head in range(key_refs[0].shape[2] // HD):
        query = stacked_query(q_ref, kv_head)
        parts = [
            masked_scores(query, ref, kv_head, first_row - (own ^ mask) * length) for ref, mask in zip(key_refs, masks)
        ]
        before = max_ref[kv_head]
        top = functools.reduce(jnp.maximum, [jnp.max(part, axis=1, keepdims=True) for part in parts])
        top = jnp.maximum(top, before[:, :1])
        weights = [jnp.exp2((part - top) * EXP_SCALE) for part in parts]
        total = sum(jnp.sum(part, axis=1, keepdims=True) for part in weights)
        factor = jnp.exp2((before - top) * EXP_SCALE)
        total_ref[kv_head] = sum_ref[kv_head] * factor + total
        scaled_ref[kv_head] = acc_ref[kv_head] * factor
        for ref, part in zip(weight_refs, weights):
            ref[kv_head] = part.astype(jnp.bfloat16)


def project(att, weight_ref, out_ref, blocks, block_width, lower):
    width = out_ref.shape[2]
    for slot, block in enumerate(blocks):
        start = pl.multiple_of(block * block_width + lower, LANES)
        out_ref[slot] = jnp.dot(
            att, weight_ref[0, :, pl.ds(start, width)], preferred_element_type=jnp.float32
        ).astype(jnp.bfloat16)


def finish_kernel(count, blocks_of, block_width, total_ref, scaled_ref, *refs):
    value_refs, weight_refs = refs[:count], refs[count : 2 * count]
    w_ref, att_ref, out_ref = refs[2 * count :]
    rows = att_ref.shape[0]
    for kv_head in range(scaled_ref.shape[0]):
        columns = slice(kv_head * HD, (kv_head + 1) * HD)
        mixed = scaled_ref[kv_head]
        for value_ref, part_ref in zip(value_refs, weight_refs):
            mixed += jnp.dot(part_ref[kv_head], value_ref[0, :, columns], preferred_element_type=jnp.float32)
        attended = (mixed / total_ref[kv_head]).astype(jnp.bfloat16)
        for g in range(G):
            head = kv_head * G + g
            att_ref[:, head * HD : (head + 1) * HD] = attended[g * rows : (g + 1) * rows]
    project(att_ref[...], w_ref, out_ref, blocks_of(lax.axis_index("tp")), block_width, 0)


def project_kernel(blocks_of, block_width, lower, att_ref, w_ref, out_ref):
    project(att_ref[...], w_ref, out_ref, blocks_of(lax.axis_index("tp")), block_width, lower)


def xor_order(lowest, size):
    if lowest >= size:
        return [0]
    rest = xor_order(lowest * 2, size)
    return [x + lowest for x in rest] + rest


def chunk_widths(width):
    units = width // LANES
    first = max(1, (2 * units) // 5)
    widths = [first, first, units - 2 * first]
    return [u * LANES for u in widths if u > 0]


def on_device(row_offsets, queries, cache_keys, cache_values, residual, out_weight):
    n_ctx, n_tp = lax.axis_size("ctx"), lax.axis_size("tp")
    rows, length = queries.shape[1], cache_keys.shape[1]
    kv_local = cache_keys.shape[2] // HD
    stacked = G * rows
    top_bit = n_ctx // 2
    block_width = out_weight.shape[2] // n_tp

    far_key = exchange(cache_keys, "ctx", top_bit)
    far_value = exchange(cache_values, "ctx", top_bit)
    near = [(0, cache_keys, cache_values)]
    bit = top_bit // 2
    while bit:
        near += [(m | bit, exchange(k, "ctx", bit), exchange(v, "ctx", bit)) for m, k, v in near]
        bit //= 2
    state = [((kv_local, stacked, HD), jnp.float32)] * 3
    half_flops = 4 * kv_local * stacked * length * HD * len(near)
    top, total, acc = local_call(
        functools.partial(early_kernel, [m for m, _, _ in near]), state, 32 * MIB, half_flops
    )(
        row_offsets, in_vmem(queries), *[in_vmem(k) for _, k, _ in near], *[in_vmem(v) for _, _, v in near]
    )
    far_keys = [(top_bit, far_key)]
    bit = top_bit // 2
    while bit:
        far_keys += [(m | bit, exchange(k, "ctx", bit)) for m, k in far_keys]
        bit //= 2
    total, scaled, *weights = local_call(
        functools.partial(late_kernel, [m for m, _ in far_keys]),
        state[:2] + [((kv_local, stacked, length), jnp.bfloat16)] * len(far_keys),
        32 * MIB,
        half_flops // 2,
    )(row_offsets, in_vmem(queries), top, total, acc, *[in_vmem(k) for _, k in far_keys])
    far_values = [far_value]
    bit = top_bit // 2
    while bit:
        far_values += [exchange(v, "ctx", bit) for v in far_values]
        bit //= 2

    order = xor_order(2, n_tp)
    keep_blocks = lambda me: [me ^ x for x in order]
    send_blocks = lambda me: [me ^ 1 ^ x for x in order]
    weight = in_vmem(out_weight)
    widths = chunk_widths(block_width)
    block_flops = 2 * rows * out_weight.shape[1] * len(order)
    attended, first_send = local_call(
        functools.partial(finish_kernel, len(far_values), send_blocks, block_width),
        [((rows, out_weight.shape[1]), jnp.bfloat16), ((len(order), rows, widths[0]), jnp.bfloat16)],
        16 * MIB,
        half_flops // 2 + block_flops * widths[0],
    )(total, scaled, *[in_vmem(v) for v in far_values], *weights, weight)

    def projected(blocks_of, lower, width):
        return local_call(
            functools.partial(project_kernel, blocks_of, block_width, lower),
            [((len(order), rows, width), jnp.bfloat16)],
            16 * MIB,
            block_flops * width,
        )(attended, weight)[0]

    outs = []
    lower = 0
    for width in widths:
        send = first_send if lower == 0 else projected(send_blocks, lower, width)
        keep = projected(keep_blocks, lower, width).astype(jnp.float32)
        bit = 1
        while bit < n_tp:
            keep = keep + exchange(send, "tp", bit).astype(jnp.float32)
            half = keep.shape[0] // 2
            send, keep = keep[:half].astype(jnp.bfloat16), keep[half:]
            bit *= 2
        updated = residual[0, :, lower : lower + width].astype(jnp.float32) + keep[0]
        outs.append(from_behind(updated.astype(jnp.bfloat16), "section", 1))
        lower += width
    return jnp.concatenate(outs, axis=1)[None]


def solution(mesh):
    placed = (
        P("section"),
        P("section", "ctx", "tp"),
        P("section", "ctx", "tp"),
        P("section", "ctx", "tp"),
        P("section", "ctx", "tp"),
        P("section", "tp", None),
    )
    return jax.shard_map(
        on_device, mesh=mesh, in_specs=placed, out_specs=P("section", "ctx", "tp"), check_vma=False
    )
```

```python
import functools
import math

import jax
import jax.numpy as jnp
from jax import lax
from jax.experimental import pallas as pl
from jax.experimental.pallas import tpu as pltpu
from jax.sharding import PartitionSpec as P

HD = 128
G = 4
LANES = 128
NEG_FILL = -1e30
MAX_FLOOR = -1e29
EXP_SCALE = HD ** (-0.5) * math.log2(math.e)
MIB = 1 << 20

WHOLE = pl.BlockSpec(memory_space=pltpu.VMEM)
IN_HBM = pl.BlockSpec(memory_space=pltpu.HBM)
SCALARS = pl.BlockSpec(memory_space=pltpu.SMEM)


def exchange(block, axis, mask):
    route = [(i, i ^ mask) for i in range(lax.axis_size(axis))]
    return lax.ppermute(block, axis, route)


def handed(block, mask):
    sections, n_tp = lax.axis_size("section"), lax.axis_size("tp")
    route = [(s * n_tp + i, (s + 1) % sections * n_tp + (i ^ mask)) for s in range(sections) for i in range(n_tp)]
    return lax.ppermute(block, ("section", "tp"), route)


def in_vmem(array):
    return pltpu.with_memory_space_constraint(array, pltpu.VMEM)


def local_call(body, ins, outs, limit, flops, scratch=()):
    return pl.pallas_call(
        body,
        in_specs=ins,
        out_shape=[pltpu.VMEM(shape, dtype) for shape, dtype in outs],
        out_specs=[WHOLE] * len(outs),
        scratch_shapes=list(scratch),
        compiler_params=pltpu.CompilerParams(vmem_limit_bytes=limit),
        cost_estimate=pl.CostEstimate(flops=0 * flops, bytes_accessed=0, transcendentals=0),
    )


def stacked_query(q_ref, kv_head):
    heads = range(kv_head * G, (kv_head + 1) * G)
    return jnp.concatenate([q_ref[0, :, h * HD : (h + 1) * HD] for h in heads], axis=0)


def masked_scores(query, key_ref, kv_head, bound):
    keys = key_ref[0, :, kv_head * HD : (kv_head + 1) * HD]
    scores = lax.dot_general(query, keys, (((1,), (1,)), ((), ())), preferred_element_type=jnp.float32)
    rows = query.shape[0] // G
    ahead = lax.broadcasted_iota(jnp.int32, scores.shape, 1) - lax.broadcasted_iota(jnp.int32, scores.shape, 0) % rows
    return jnp.where(ahead <= bound, scores, NEG_FILL)


def early_kernel(masks, offset_ref, q_hbm, key_hbm, value_hbm, w_hbm, *refs):
    count = len(masks)
    key_refs, value_refs = list(refs[: count - 1]), list(refs[count - 1 : 2 * count - 2])
    max_ref, sum_ref, acc_ref, query_ref, w_ref, q_ref, key_ref, value_ref, sems = refs[2 * count - 2 :]
    sources = (q_hbm, key_hbm, value_hbm, w_hbm)
    targets = (q_ref, key_ref, value_ref, w_ref)
    copies = [pltpu.make_async_copy(a, b, sems.at[i]) for i, (a, b) in enumerate(zip(sources, targets))]
    for copy in copies:
        copy.start()
    for copy in copies[:3]:
        copy.wait()
    key_refs, value_refs = [key_ref] + key_refs, [value_ref] + value_refs
    own = lax.axis_index("ctx")
    rows, length = q_ref.shape[1], key_refs[0].shape[1]
    first_row = offset_ref[0] + own * rows
    for kv_head in range(key_refs[0].shape[2] // HD):
        columns = slice(kv_head * HD, (kv_head + 1) * HD)
        query = stacked_query(q_ref, kv_head)
        query_ref[kv_head] = query
        parts = [
            masked_scores(query, ref, kv_head, first_row - (own ^ mask) * length) for ref, mask in zip(key_refs, masks)
        ]
        top = functools.reduce(jnp.maximum, [jnp.max(part, axis=1, keepdims=True) for part in parts])
        top = jnp.maximum(top, MAX_FLOOR)
        weights = [jnp.exp2((part - top) * EXP_SCALE) for part in parts]
        total = sum(jnp.sum(part, axis=1, keepdims=True) for part in weights)
        mixed = sum(
            jnp.dot(part.astype(jnp.bfloat16), ref[0, :, columns], preferred_element_type=jnp.float32)
            for part, ref in zip(weights, value_refs)
        )
        max_ref[kv_head] = jnp.broadcast_to(top, max_ref.shape[1:])
        sum_ref[kv_head] = jnp.broadcast_to(total, sum_ref.shape[1:])
        acc_ref[kv_head] = mixed
    copies[3].wait()


def late_kernel(masks, offset_ref, q_ref, max_ref, sum_ref, acc_ref, *refs):
    count = len(masks)
    key_refs, refs = refs[:count], refs[count:]
    outs = refs[-(3 + count) :]
    before_refs = refs[: -(3 + count)]
    top_ref, total_ref, scaled_ref = outs[:3]
    weight_refs = outs[3:]
    own = lax.axis_index("ctx")
    rows, length = q_ref.shape[1] // G, key_refs[0].shape[1]
    first_row = offset_ref[0] + own * rows
    for kv_head in range(key_refs[0].shape[2] // HD):
        columns = slice(kv_head * HD, (kv_head + 1) * HD)
        parts = [
            masked_scores(q_ref[kv_head], ref, kv_head, first_row - (own ^ mask) * length)
            for ref, mask in zip(key_refs, masks)
        ]
        before = max_ref[kv_head]
        top = functools.reduce(jnp.maximum, [jnp.max(part, axis=1, keepdims=True) for part in parts])
        top = jnp.maximum(top, before[:, :1])
        weights = [jnp.exp2((part - top) * EXP_SCALE) for part in parts]
        total = sum(jnp.sum(part, axis=1, keepdims=True) for part in weights)
        factor = jnp.exp2((before - top) * EXP_SCALE)
        mixed = acc_ref[kv_head]
        if before_refs:
            mixed += jnp.dot(
                before_refs[0][kv_head], before_refs[1][0, :, columns], preferred_element_type=jnp.float32
            )
        top_ref[kv_head] = jnp.broadcast_to(top, before.shape)
        total_ref[kv_head] = sum_ref[kv_head] * factor + total
        scaled_ref[kv_head] = mixed * factor
        for ref, part in zip(weight_refs, weights):
            ref[kv_head] = part.astype(jnp.bfloat16)


def project(att, weight_ref, out_refs, blocks, block_width, lower):
    slots = []
    for ref in out_refs:
        slots += [ref.at[i] for i in range(ref.shape[0])] if len(ref.shape) == 3 else [ref]
    for ref, block in zip(slots, blocks):
        start = pl.multiple_of(block * block_width + lower, LANES)
        ref[...] = jnp.dot(
            att, weight_ref[0, :, pl.ds(start, ref.shape[1])], preferred_element_type=jnp.float32
        ).astype(jnp.bfloat16)


def finish_kernel(count, blocks_of, block_width, lower, total_ref, scaled_ref, *refs):
    value_refs, weight_refs = refs[:count], refs[count : 2 * count]
    w_ref, att_ref, out_ref = refs[2 * count :]
    rows = att_ref.shape[0]
    for kv_head in range(scaled_ref.shape[0]):
        columns = slice(kv_head * HD, (kv_head + 1) * HD)
        mixed = scaled_ref[kv_head]
        for value_ref, part_ref in zip(value_refs, weight_refs):
            mixed += jnp.dot(part_ref[kv_head], value_ref[0, :, columns], preferred_element_type=jnp.float32)
        attended = (mixed / total_ref[kv_head]).astype(jnp.bfloat16)
        for g in range(G):
            head = kv_head * G + g
            att_ref[:, head * HD : (head + 1) * HD] = attended[g * rows : (g + 1) * rows]
    project(att_ref[...], w_ref, [out_ref], blocks_of(lax.axis_index("tp")), block_width, lower)


def project_kernel(blocks_of, block_width, lower, att_ref, w_ref, *out_refs):
    project(att_ref[...], w_ref, out_refs, blocks_of(lax.axis_index("tp")), block_width, lower)


def xor_order(lowest, size):
    if lowest >= size:
        return [0]
    rest = xor_order(lowest * 2, size)
    return [x + lowest for x in rest] + rest


def chunk_plan(width):
    units = width // LANES
    first = (units + 1) // 2
    return [u * LANES for u in (first, units - first) if u > 0]


def on_device(row_offsets, queries, cache_keys, cache_values, residual, out_weight):
    n_ctx, n_tp = lax.axis_size("ctx"), lax.axis_size("tp")
    rows, length = queries.shape[1], cache_keys.shape[1]
    kv_local = cache_keys.shape[2] // HD
    stacked = G * rows
    top_bit = n_ctx // 2
    block_width = out_weight.shape[2] // n_tp

    far_key = exchange(cache_keys, "ctx", top_bit)
    far_value = exchange(cache_values, "ctx", top_bit)
    near = [(0, cache_keys, cache_values)]
    bit = top_bit // 2
    while bit:
        near += [(m | bit, exchange(k, "ctx", bit), exchange(v, "ctx", bit)) for m, k, v in near]
        bit //= 2
    state = [((kv_local, stacked, HD), jnp.float32)] * 3
    half_flops = 4 * kv_local * stacked * length * HD * len(near)
    local = [queries, cache_keys, cache_values, out_weight]
    top, total, acc, query, weight = local_call(
        functools.partial(early_kernel, [m for m, _, _ in near]),
        [SCALARS] + [IN_HBM] * 4 + [WHOLE] * (2 * len(near) - 2),
        state + [((kv_local, stacked, HD), jnp.bfloat16), (out_weight.shape, out_weight.dtype)],
        32 * MIB,
        half_flops,
        [pltpu.VMEM(a.shape, a.dtype) for a in local[:3]] + [pltpu.SemaphoreType.DMA((4,))],
    )(
        row_offsets,
        *[pltpu.with_memory_space_constraint(a, pltpu.HBM) for a in local],
        *[in_vmem(k) for _, k, _ in near[1:]],
        *[in_vmem(v) for _, _, v in near[1:]],
    )
    near_key, top = lax.optimization_barrier((far_key, top))
    far_keys = [(top_bit, near_key)]
    bit = top_bit // 2
    while bit:
        far_keys += [(m | bit, exchange(k, "ctx", bit)) for m, k in far_keys]
        bit //= 2

    def late(masks, outs, *operands):
        return local_call(
            functools.partial(late_kernel, masks),
            [SCALARS] + [WHOLE] * len(operands),
            state + [((kv_local, stacked, length), jnp.bfloat16)] * len(masks),
            32 * MIB,
            half_flops,
        )(row_offsets, *operands)

    top, total, acc, far_weights = late([top_bit], 0, query, top, total, acc, in_vmem(far_key))
    far_value, total = lax.optimization_barrier((far_value, total))
    far_values = [far_value]
    bit = top_bit // 2
    while bit:
        far_values += [exchange(v, "ctx", bit) for v in far_values]
        bit //= 2
    masks, keys = zip(*far_keys[1:])
    top, total, acc, *weights = late(
        list(masks), 0, query, top, total, acc, *[in_vmem(k) for k in keys], far_weights, in_vmem(far_value)
    )
    far_values = far_values[1:]

    order = xor_order(2, n_tp)
    across = order[:-1]
    widths = chunk_plan(block_width)
    lowers = [sum(widths[:i]) for i in range(len(widths))]
    block_flops = 2 * rows * out_weight.shape[1]
    attended, send = local_call(
        functools.partial(finish_kernel, len(far_values), lambda me: [me ^ 1 ^ x for x in across], block_width, 0),
        [WHOLE] * (3 + 2 * len(far_values)),
        [((rows, out_weight.shape[1]), jnp.bfloat16), ((len(across), rows, widths[0]), jnp.bfloat16)],
        16 * MIB,
        half_flops // 2 + block_flops * widths[0] * len(across),
    )(total, acc, *[in_vmem(v) for v in far_values], *weights, weight)

    def projected(masks, lower, width, stack=False):
        shapes = [((len(masks), rows, width), jnp.bfloat16)] if stack else [((rows, width), jnp.bfloat16)] * len(masks)
        return local_call(
            functools.partial(project_kernel, lambda me: [me ^ x for x in masks], block_width, lower),
            [WHOLE] * 2,
            shapes,
            16 * MIB,
            block_flops * width * len(masks),
        )(attended, weight)

    firsts = []
    for lower, width in zip(lowers, widths):
        if lower:
            (send,) = projected([1 ^ x for x in across], lower, width, True)
        firsts.append(exchange(send, "tp", 1))
    pair, own = projected([1, 0], 0, block_width)
    kept = [projected(across, lower, width) for lower, width in zip(lowers, widths)]
    own = (own.astype(jnp.float32) + residual[0].astype(jnp.float32)).astype(jnp.bfloat16)
    whole = [handed(own, 0), handed(pair, 1)]
    outs = []
    for lower, width, first, part in zip(lowers, widths, firsts, kept):
        part = [a.astype(jnp.float32) + first[i].astype(jnp.float32) for i, a in enumerate(part)]
        terms = [a[:, lower : lower + width] for a in whole]
        bit = 2
        while bit < n_tp:
            half = (len(part) + 1) // 2
            sends = [a.astype(jnp.bfloat16) for a in part[:half]]
            received = [exchange(a, "tp", bit) for a in sends[:-1]]
            terms.append(handed(sends[-1], bit))
            part = [a + r.astype(jnp.float32) for a, r in zip(part[half:], received)]
            bit *= 2
        outs.append(sum(term.astype(jnp.float32) for term in terms).astype(jnp.bfloat16))
    return jnp.concatenate(outs, axis=1)[None]


def solution(mesh):
    placed = (
        P("section"),
        P("section", "ctx", "tp"),
        P("section", "ctx", "tp"),
        P("section", "ctx", "tp"),
        P("section", "ctx", "tp"),
        P("section", "tp", None),
    )
    return jax.shard_map(
        on_device, mesh=mesh, in_specs=placed, out_specs=P("section", "ctx", "tp"), check_vma=False
    )
```

```python
import functools
import math

import jax
import jax.numpy as jnp
from jax import lax
from jax.experimental import pallas as pl
from jax.experimental.pallas import tpu as pltpu
from jax.sharding import PartitionSpec as P

HD = 128
G = 4
LANES = 128
NEG_FILL = -1e30
MAX_FLOOR = -1e29
EXP_SCALE = HD ** (-0.5) * math.log2(math.e)
MIB = 1 << 20

WHOLE = pl.BlockSpec(memory_space=pltpu.VMEM)
IN_HBM = pl.BlockSpec(memory_space=pltpu.HBM)
SCALARS = pl.BlockSpec(memory_space=pltpu.SMEM)


def exchange(block, axis, mask):
    route = [(i, i ^ mask) for i in range(lax.axis_size(axis))]
    return lax.ppermute(block, axis, route)


def handed(block, mask):
    sections, n_tp = lax.axis_size("section"), lax.axis_size("tp")
    route = [(s * n_tp + i, (s + 1) % sections * n_tp + (i ^ mask)) for s in range(sections) for i in range(n_tp)]
    return lax.ppermute(block, ("section", "tp"), route)


def in_vmem(array):
    return pltpu.with_memory_space_constraint(array, pltpu.VMEM)


def local_call(body, ins, outs, limit, flops, scratch=()):
    return pl.pallas_call(
        body,
        in_specs=ins,
        out_shape=[pltpu.VMEM(shape, dtype) for shape, dtype in outs],
        out_specs=[WHOLE] * len(outs),
        scratch_shapes=list(scratch),
        compiler_params=pltpu.CompilerParams(vmem_limit_bytes=limit),
        cost_estimate=pl.CostEstimate(flops=flops, bytes_accessed=0, transcendentals=0),
    )


def stacked_query(q_ref, kv_head):
    heads = range(kv_head * G, (kv_head + 1) * G)
    return jnp.concatenate([q_ref[0, :, h * HD : (h + 1) * HD] for h in heads], axis=0)


def masked_scores(query, key_ref, kv_head, bound):
    keys = key_ref[0, :, kv_head * HD : (kv_head + 1) * HD]
    scores = lax.dot_general(query, keys, (((1,), (1,)), ((), ())), preferred_element_type=jnp.float32)
    rows = query.shape[0] // G
    ahead = lax.broadcasted_iota(jnp.int32, scores.shape, 1) - lax.broadcasted_iota(jnp.int32, scores.shape, 0) % rows
    return jnp.where(ahead <= bound, scores, NEG_FILL)


def early_kernel(masks, offset_ref, q_hbm, key_hbm, value_hbm, w_hbm, *refs):
    count = len(masks)
    key_refs, value_refs = list(refs[: count - 1]), list(refs[count - 1 : 2 * count - 2])
    max_ref, sum_ref, acc_ref, query_ref, w_ref, q_ref, key_ref, value_ref, sems = refs[2 * count - 2 :]
    sources = (q_hbm, key_hbm, value_hbm, w_hbm)
    targets = (q_ref, key_ref, value_ref, w_ref)
    copies = [pltpu.make_async_copy(a, b, sems.at[i]) for i, (a, b) in enumerate(zip(sources, targets))]
    for copy in copies:
        copy.start()
    for copy in copies[:3]:
        copy.wait()
    key_refs, value_refs = [key_ref] + key_refs, [value_ref] + value_refs
    own = lax.axis_index("ctx")
    rows, length = q_ref.shape[1], key_refs[0].shape[1]
    first_row = offset_ref[0] + own * rows
    for kv_head in range(key_refs[0].shape[2] // HD):
        columns = slice(kv_head * HD, (kv_head + 1) * HD)
        query = stacked_query(q_ref, kv_head)
        query_ref[kv_head] = query
        parts = [
            masked_scores(query, ref, kv_head, first_row - (own ^ mask) * length) for ref, mask in zip(key_refs, masks)
        ]
        top = functools.reduce(jnp.maximum, [jnp.max(part, axis=1, keepdims=True) for part in parts])
        top = jnp.maximum(top, MAX_FLOOR)
        weights = [jnp.exp2((part - top) * EXP_SCALE) for part in parts]
        total = sum(jnp.sum(part, axis=1, keepdims=True) for part in weights)
        mixed = sum(
            jnp.dot(part.astype(jnp.bfloat16), ref[0, :, columns], preferred_element_type=jnp.float32)
            for part, ref in zip(weights, value_refs)
        )
        max_ref[kv_head] = jnp.broadcast_to(top, max_ref.shape[1:])
        sum_ref[kv_head] = jnp.broadcast_to(total, sum_ref.shape[1:])
        acc_ref[kv_head] = mixed
    copies[3].wait()


def late_kernel(masks, offset_ref, q_ref, max_ref, sum_ref, acc_ref, *refs):
    count = len(masks)
    key_refs, refs = refs[:count], refs[count:]
    top_ref, total_ref, scaled_ref = refs[:3]
    weight_refs = refs[3:]
    own = lax.axis_index("ctx")
    rows, length = q_ref.shape[1] // G, key_refs[0].shape[1]
    first_row = offset_ref[0] + own * rows
    for kv_head in range(key_refs[0].shape[2] // HD):
        parts = [
            masked_scores(q_ref[kv_head], ref, kv_head, first_row - (own ^ mask) * length)
            for ref, mask in zip(key_refs, masks)
        ]
        before = max_ref[kv_head]
        top = functools.reduce(jnp.maximum, [jnp.max(part, axis=1, keepdims=True) for part in parts])
        top = jnp.maximum(top, before[:, :1])
        weights = [jnp.exp2((part - top) * EXP_SCALE) for part in parts]
        total = sum(jnp.sum(part, axis=1, keepdims=True) for part in weights)
        factor = jnp.exp2((before - top) * EXP_SCALE)
        top_ref[kv_head] = jnp.broadcast_to(top, before.shape)
        total_ref[kv_head] = sum_ref[kv_head] * factor + total
        scaled_ref[kv_head] = acc_ref[kv_head] * factor
        for ref, part in zip(weight_refs, weights):
            ref[kv_head] = part.astype(jnp.bfloat16)


def finish_kernel(count, block_width, before_ref, top_ref, total_ref, acc_ref, residual_ref, w_ref, *refs):
    value_refs, weight_refs = refs[:count], refs[count : 2 * count]
    att_ref, own_ref = refs[2 * count :]
    rows = att_ref.shape[0]
    for kv_head in range(acc_ref.shape[0]):
        columns = slice(kv_head * HD, (kv_head + 1) * HD)
        parts = [
            jnp.dot(part_ref[kv_head], value_ref[0, :, columns], preferred_element_type=jnp.float32)
            for value_ref, part_ref in zip(value_refs, weight_refs)
        ]
        factor = jnp.exp2((before_ref[kv_head] - top_ref[kv_head]) * EXP_SCALE)
        mixed = acc_ref[kv_head] + parts[0] * factor + sum(parts[1:])
        attended = (mixed / total_ref[kv_head]).astype(jnp.bfloat16)
        for g in range(G):
            head = kv_head * G + g
            att_ref[:, head * HD : (head + 1) * HD] = attended[g * rows : (g + 1) * rows]
    start = pl.multiple_of(lax.axis_index("tp") * block_width, LANES)
    width = own_ref.shape[1]
    own = jnp.dot(att_ref[...], w_ref[0, :, pl.ds(start, width)], preferred_element_type=jnp.float32)
    own_ref[...] = (residual_ref[0, :, :width].astype(jnp.float32) + own).astype(jnp.bfloat16)


def project_kernel(groups, block_width, att_ref, w_ref, *out_refs):
    me = lax.axis_index("tp")
    for (xs, lower, width), out_ref in zip(groups, out_refs):
        for slot, x in enumerate(xs):
            start = pl.multiple_of((me ^ x) * block_width + lower, LANES)
            out_ref[slot] = jnp.dot(
                att_ref[...], w_ref[0, :, pl.ds(start, width)], preferred_element_type=jnp.float32
            ).astype(jnp.bfloat16)


def xor_order(lowest, size):
    if lowest >= size:
        return [0]
    rest = xor_order(lowest * 2, size)
    return [x + lowest for x in rest] + rest


def cross_first_width(width):
    return max(1, (2 * (width // LANES)) // 10) * LANES


def on_device(row_offsets, queries, cache_keys, cache_values, residual, out_weight):
    n_ctx, n_tp = lax.axis_size("ctx"), lax.axis_size("tp")
    rows, length = queries.shape[1], cache_keys.shape[1]
    kv_local = cache_keys.shape[2] // HD
    stacked = G * rows
    top_bit = n_ctx // 2
    block_width = out_weight.shape[2] // n_tp

    far_key = exchange(cache_keys, "ctx", top_bit)
    far_value = exchange(cache_values, "ctx", top_bit)
    near = [(0, cache_keys, cache_values)]
    bit = top_bit // 2
    while bit:
        near += [(m | bit, exchange(k, "ctx", bit), exchange(v, "ctx", bit)) for m, k, v in near]
        bit //= 2
    state = [((kv_local, stacked, HD), jnp.float32)] * 3
    half_flops = 4 * kv_local * stacked * length * HD * len(near)
    local = [queries, cache_keys, cache_values, out_weight]
    top, total, acc, query, weight = local_call(
        functools.partial(early_kernel, [m for m, _, _ in near]),
        [SCALARS] + [IN_HBM] * 4 + [WHOLE] * (2 * len(near) - 2),
        state + [((kv_local, stacked, HD), jnp.bfloat16), (out_weight.shape, out_weight.dtype)],
        32 * MIB,
        0,
        [pltpu.VMEM(a.shape, a.dtype) for a in local[:3]] + [pltpu.SemaphoreType.DMA((4,))],
    )(
        row_offsets,
        *[pltpu.with_memory_space_constraint(a, pltpu.HBM) for a in local],
        *[in_vmem(k) for _, k, _ in near[1:]],
        *[in_vmem(v) for _, _, v in near[1:]],
    )
    near_key, top = lax.optimization_barrier((far_key, top))
    far_keys = [(top_bit, near_key)]
    bit = top_bit // 2
    while bit:
        far_keys += [(m | bit, exchange(k, "ctx", bit)) for m, k in far_keys]
        bit //= 2

    def late(masks, outs, *operands):
        return local_call(
            functools.partial(late_kernel, masks),
            [SCALARS] + [WHOLE] * len(operands),
            state + [((kv_local, stacked, length), jnp.bfloat16)] * len(masks),
            32 * MIB,
            0,
        )(row_offsets, *operands)

    near_top, total, acc, far_weights = late([top_bit], 0, query, top, total, acc, in_vmem(far_key))
    far_value, total = lax.optimization_barrier((far_value, total))
    far_values = [far_value]
    bit = top_bit // 2
    while bit:
        far_values += [exchange(v, "ctx", bit) for v in far_values]
        bit //= 2
    masks, keys = zip(*far_keys[1:])
    top, total, acc, *weights = late(list(masks), 0, query, near_top, total, acc, *[in_vmem(k) for k in keys])
    weights = [far_weights, *weights]

    across = xor_order(2, n_tp)[:-1]
    cross_width = cross_first_width(block_width)
    pair_width = block_width - cross_width
    block_flops = 2 * rows * out_weight.shape[1]
    attended, own_a = local_call(
        functools.partial(finish_kernel, len(far_values), block_width),
        [WHOLE] * (6 + 2 * len(far_values)),
        [((rows, out_weight.shape[1]), jnp.bfloat16), ((rows, pair_width), jnp.bfloat16)],
        16 * MIB,
        0,
    )(near_top, top, total, acc, in_vmem(residual), weight, *[in_vmem(v) for v in far_values], *weights)

    def projected(*groups):
        return local_call(
            functools.partial(project_kernel, groups, block_width),
            [WHOLE] * 2,
            [((len(xs), rows, width), jnp.bfloat16) for xs, _, width in groups],
            16 * MIB,
            block_flops * sum(len(xs) * width for xs, _, width in groups),
        )(attended, weight)

    half = n_tp // 2
    own_a = handed(own_a, 0)
    (send_a,) = projected(([1 ^ x for x in across], 0, pair_width))
    send_b, pair_a = projected((list(range(half, n_tp)), pair_width, cross_width), ([1], 0, pair_width))
    kept_a, kept_b = projected((across, 0, pair_width), (list(range(half)), pair_width, cross_width))
    got_a = exchange(send_a, "tp", 1)
    got_b = exchange(send_b, "tp", half)
    pair_a = handed(pair_a[0], 1)
    own_a, got_a = lax.optimization_barrier((own_a, got_a))

    part = [kept_a[i].astype(jnp.float32) + got_a[i].astype(jnp.float32) for i in range(len(across))]
    terms_a = [own_a, pair_a]
    bit = 2
    while bit < n_tp:
        count = (len(part) + 1) // 2
        sends = [a.astype(jnp.bfloat16) for a in part[:count]]
        received = [exchange(a, "tp", bit) for a in sends[:-1]]
        terms_a.append(handed(sends[-1], bit))
        part = [a + r.astype(jnp.float32) for a, r in zip(part[count:], received)]
        bit *= 2

    part = [kept_b[i].astype(jnp.float32) + got_b[i].astype(jnp.float32) for i in range(half)]
    while len(part) > 2:
        count = len(part) // 2
        received = [exchange(a.astype(jnp.bfloat16), "tp", count) for a in part[count:]]
        part = [a + r.astype(jnp.float32) for a, r in zip(part[:count], received)]
    part[0] = part[0] + residual[0, :, pair_width:].astype(jnp.float32)
    part = [a.astype(jnp.bfloat16) for a in part]
    terms_b = [handed(a, x) for x, a in enumerate(part)]

    def total_of(terms):
        return sum(term.astype(jnp.float32) for term in terms).astype(jnp.bfloat16)

    total_a = total_of(terms_a)
    total_a, *terms_b = lax.optimization_barrier((total_a, *terms_b))
    return jnp.concatenate([total_a, total_of(terms_b)], axis=1)[None]


def solution(mesh):
    placed = (
        P("section"),
        P("section", "ctx", "tp"),
        P("section", "ctx", "tp"),
        P("section", "ctx", "tp"),
        P("section", "ctx", "tp"),
        P("section", "tp", None),
    )
    return jax.shard_map(
        on_device, mesh=mesh, in_specs=placed, out_specs=P("section", "ctx", "tp"), check_vma=False
    )
```

```python
import functools
import math

import jax
import jax.numpy as jnp
from jax import lax
from jax.experimental import pallas as pl
from jax.experimental.pallas import tpu as pltpu
from jax.sharding import PartitionSpec as P

HD = 128
G = 4
LANES = 128
NEG_FILL = -1e30
MAX_FLOOR = -1e29
EXP_SCALE = HD ** (-0.5) * math.log2(math.e)
MIB = 1 << 20

WHOLE = pl.BlockSpec(memory_space=pltpu.VMEM)
IN_HBM = pl.BlockSpec(memory_space=pltpu.HBM)
SCALARS = pl.BlockSpec(memory_space=pltpu.SMEM)


def exchange(block, axis, mask):
    route = [(i, i ^ mask) for i in range(lax.axis_size(axis))]
    return lax.ppermute(block, axis, route)


def handed(block, mask):
    sections, n_tp = lax.axis_size("section"), lax.axis_size("tp")
    route = [(s * n_tp + i, (s + 1) % sections * n_tp + (i ^ mask)) for s in range(sections) for i in range(n_tp)]
    return lax.ppermute(block, ("section", "tp"), route)


def in_vmem(array):
    return pltpu.with_memory_space_constraint(array, pltpu.VMEM)


def local_call(body, ins, outs, limit, flops, scratch=()):
    return pl.pallas_call(
        body,
        in_specs=ins,
        out_shape=[pltpu.VMEM(shape, dtype) for shape, dtype in outs],
        out_specs=[WHOLE] * len(outs),
        scratch_shapes=list(scratch),
        compiler_params=pltpu.CompilerParams(vmem_limit_bytes=limit),
        cost_estimate=pl.CostEstimate(flops=flops, bytes_accessed=0, transcendentals=0),
    )


def stacked_query(q_ref, kv_head):
    heads = range(kv_head * G, (kv_head + 1) * G)
    return jnp.concatenate([q_ref[0, :, h * HD : (h + 1) * HD] for h in heads], axis=0)


def masked_scores(query, key_ref, kv_head, bound):
    keys = key_ref[0, :, kv_head * HD : (kv_head + 1) * HD]
    scores = lax.dot_general(query, keys, (((1,), (1,)), ((), ())), preferred_element_type=jnp.float32)
    rows = query.shape[0] // G
    ahead = lax.broadcasted_iota(jnp.int32, scores.shape, 1) - lax.broadcasted_iota(jnp.int32, scores.shape, 0) % rows
    return jnp.where(ahead <= bound, scores, NEG_FILL)


def early_kernel(masks, offset_ref, q_hbm, key_hbm, value_hbm, w_hbm, *refs):
    count = len(masks)
    key_refs, value_refs = list(refs[: count - 1]), list(refs[count - 1 : 2 * count - 2])
    max_ref, sum_ref, acc_ref, query_ref, w_ref, q_ref, key_ref, value_ref, sems = refs[2 * count - 2 :]
    sources = (q_hbm, key_hbm, value_hbm, w_hbm)
    targets = (q_ref, key_ref, value_ref, w_ref)
    copies = [pltpu.make_async_copy(a, b, sems.at[i]) for i, (a, b) in enumerate(zip(sources, targets))]
    for copy in copies:
        copy.start()
    for copy in copies[:3]:
        copy.wait()
    key_refs, value_refs = [key_ref] + key_refs, [value_ref] + value_refs
    own = lax.axis_index("ctx")
    rows, length = q_ref.shape[1], key_refs[0].shape[1]
    first_row = offset_ref[0] + own * rows
    for kv_head in range(key_refs[0].shape[2] // HD):
        columns = slice(kv_head * HD, (kv_head + 1) * HD)
        query = stacked_query(q_ref, kv_head)
        query_ref[kv_head] = query
        parts = [
            masked_scores(query, ref, kv_head, first_row - (own ^ mask) * length) for ref, mask in zip(key_refs, masks)
        ]
        top = functools.reduce(jnp.maximum, [jnp.max(part, axis=1, keepdims=True) for part in parts])
        top = jnp.maximum(top, MAX_FLOOR)
        weights = [jnp.exp2((part - top) * EXP_SCALE) for part in parts]
        total = sum(jnp.sum(part, axis=1, keepdims=True) for part in weights)
        mixed = sum(
            jnp.dot(part.astype(jnp.bfloat16), ref[0, :, columns], preferred_element_type=jnp.float32)
            for part, ref in zip(weights, value_refs)
        )
        max_ref[kv_head] = jnp.broadcast_to(top, max_ref.shape[1:])
        sum_ref[kv_head] = jnp.broadcast_to(total, sum_ref.shape[1:])
        acc_ref[kv_head] = mixed
    copies[3].wait()


def late_kernel(masks, offset_ref, q_ref, max_ref, sum_ref, acc_ref, *refs):
    count = len(masks)
    key_refs, refs = refs[:count], refs[count:]
    top_ref, total_ref, scaled_ref = refs[:3]
    weight_refs = refs[3:]
    own = lax.axis_index("ctx")
    rows, length = q_ref.shape[1] // G, key_refs[0].shape[1]
    first_row = offset_ref[0] + own * rows
    for kv_head in range(key_refs[0].shape[2] // HD):
        parts = [
            masked_scores(q_ref[kv_head], ref, kv_head, first_row - (own ^ mask) * length)
            for ref, mask in zip(key_refs, masks)
        ]
        before = max_ref[kv_head]
        top = functools.reduce(jnp.maximum, [jnp.max(part, axis=1, keepdims=True) for part in parts])
        top = jnp.maximum(top, before[:, :1])
        weights = [jnp.exp2((part - top) * EXP_SCALE) for part in parts]
        total = sum(jnp.sum(part, axis=1, keepdims=True) for part in weights)
        factor = jnp.exp2((before - top) * EXP_SCALE)
        top_ref[kv_head] = jnp.broadcast_to(top, before.shape)
        total_ref[kv_head] = sum_ref[kv_head] * factor + total
        scaled_ref[kv_head] = acc_ref[kv_head] * factor
        for ref, part in zip(weight_refs, weights):
            ref[kv_head] = part.astype(jnp.bfloat16)


def project_blocks(att_ref, w_ref, block_width, group, out_ref):
    xs, lower, width = group
    for slot, x in enumerate(xs):
        start = pl.multiple_of((lax.axis_index("tp") ^ x) * block_width + lower, LANES)
        out_ref[slot] = jnp.dot(
            att_ref[...], w_ref[0, :, pl.ds(start, width)], preferred_element_type=jnp.float32
        ).astype(jnp.bfloat16)


def finish_kernel(count, block_width, group, before_ref, top_ref, total_ref, acc_ref, w_ref, *refs):
    value_refs, weight_refs = refs[:count], refs[count : 2 * count]
    att_ref, send_ref = refs[2 * count :]
    rows = att_ref.shape[0]
    for kv_head in range(acc_ref.shape[0]):
        columns = slice(kv_head * HD, (kv_head + 1) * HD)
        parts = [
            jnp.dot(part_ref[kv_head], value_ref[0, :, columns], preferred_element_type=jnp.float32)
            for value_ref, part_ref in zip(value_refs, weight_refs)
        ]
        factor = jnp.exp2((before_ref[kv_head] - top_ref[kv_head]) * EXP_SCALE)
        mixed = acc_ref[kv_head] + parts[0] * factor + sum(parts[1:])
        attended = (mixed / total_ref[kv_head]).astype(jnp.bfloat16)
        for g in range(G):
            head = kv_head * G + g
            att_ref[:, head * HD : (head + 1) * HD] = attended[g * rows : (g + 1) * rows]
    project_blocks(att_ref, w_ref, block_width, group, send_ref)


def own_kernel(block_width, att_ref, w_ref, residual_ref, own_ref):
    start = pl.multiple_of(lax.axis_index("tp") * block_width, LANES)
    width = own_ref.shape[1]
    own = jnp.dot(att_ref[...], w_ref[0, :, pl.ds(start, width)], preferred_element_type=jnp.float32)
    own_ref[...] = (residual_ref[0, :, :width].astype(jnp.float32) + own).astype(jnp.bfloat16)


def project_kernel(groups, block_width, att_ref, w_ref, *out_refs):
    for group, out_ref in zip(groups, out_refs):
        project_blocks(att_ref, w_ref, block_width, group, out_ref)


def total_kernel(count, *refs):
    *term_refs, out_ref, total_ref, sems = refs
    lower = term_refs[0].shape[1]
    half = out_ref.shape[0] // 2
    copies = []
    for i, rows in enumerate((slice(0, half), slice(half, 2 * half))):
        for group, columns in ((term_refs[:count], slice(0, lower)), (term_refs[count:], slice(lower, None))):
            total_ref[rows, columns] = sum(ref[rows].astype(jnp.float32) for ref in group).astype(jnp.bfloat16)
        copies.append(pltpu.make_async_copy(total_ref.at[rows], out_ref.at[rows], sems.at[i]))
        copies[-1].start()
    for copy in copies:
        copy.wait()


def xor_order(lowest, size):
    if lowest >= size:
        return [0]
    rest = xor_order(lowest * 2, size)
    return [x + lowest for x in rest] + rest


def cross_first_width(width):
    return max(1, (2 * (width // LANES)) // 10) * LANES


def on_device(row_offsets, queries, cache_keys, cache_values, residual, out_weight):
    n_ctx, n_tp = lax.axis_size("ctx"), lax.axis_size("tp")
    rows, length = queries.shape[1], cache_keys.shape[1]
    kv_local = cache_keys.shape[2] // HD
    stacked = G * rows
    top_bit = n_ctx // 2
    block_width = out_weight.shape[2] // n_tp

    far_key = exchange(cache_keys, "ctx", top_bit)
    far_value = exchange(cache_values, "ctx", top_bit)
    near = [(0, cache_keys, cache_values)]
    bit = top_bit // 2
    while bit:
        near += [(m | bit, exchange(k, "ctx", bit), exchange(v, "ctx", bit)) for m, k, v in near]
        bit //= 2
    state = [((kv_local, stacked, HD), jnp.float32)] * 3
    half_flops = 4 * kv_local * stacked * length * HD * len(near)
    local = [queries, cache_keys, cache_values, out_weight]
    masks, keys, values = zip(*near)
    far_key, keys, values = lax.optimization_barrier((far_key, keys, values))
    near = list(zip(masks, keys, values))
    top, total, acc, query, weight = local_call(
        functools.partial(early_kernel, [m for m, _, _ in near]),
        [SCALARS] + [IN_HBM] * 4 + [WHOLE] * (2 * len(near) - 2),
        state + [((kv_local, stacked, HD), jnp.bfloat16), (out_weight.shape, out_weight.dtype)],
        32 * MIB,
        0,
        [pltpu.VMEM(a.shape, a.dtype) for a in local[:3]] + [pltpu.SemaphoreType.DMA((4,))],
    )(
        row_offsets,
        *[pltpu.with_memory_space_constraint(a, pltpu.HBM) for a in local],
        *[in_vmem(k) for _, k, _ in near[1:]],
        *[in_vmem(v) for _, _, v in near[1:]],
    )
    near_key, top = lax.optimization_barrier((far_key, top))
    far_keys = [(top_bit, near_key)]
    bit = top_bit // 2
    while bit:
        far_keys += [(m | bit, exchange(k, "ctx", bit)) for m, k in far_keys]
        bit //= 2

    def late(masks, outs, *operands):
        return local_call(
            functools.partial(late_kernel, masks),
            [SCALARS] + [WHOLE] * len(operands),
            state + [((kv_local, stacked, length), jnp.bfloat16)] * len(masks),
            32 * MIB,
            0,
        )(row_offsets, *operands)

    near_top, total, acc, far_weights = late([top_bit], 0, query, top, total, acc, in_vmem(far_key))
    far_value, total = lax.optimization_barrier((far_value, total))
    far_values = [far_value]
    bit = top_bit // 2
    while bit:
        far_values += [exchange(v, "ctx", bit) for v in far_values]
        bit //= 2
    masks, keys = zip(*far_keys[1:])
    top, total, acc, *weights = late(list(masks), 0, query, near_top, total, acc, *[in_vmem(k) for k in keys])
    weights = [far_weights, *weights]

    across = xor_order(2, n_tp)[:-1]
    cross_width = cross_first_width(block_width)
    pair_width = block_width - cross_width
    block_flops = 2 * rows * out_weight.shape[1]
    relay = ([1 ^ x for x in across], 0, pair_width)
    attended, send_a = local_call(
        functools.partial(finish_kernel, len(far_values), block_width, relay),
        [WHOLE] * (5 + 2 * len(far_values)),
        [((rows, out_weight.shape[1]), jnp.bfloat16), ((len(across), rows, pair_width), jnp.bfloat16)],
        16 * MIB,
        0,
    )(near_top, top, total, acc, weight, *[in_vmem(v) for v in far_values], *weights)
    (own_a,) = local_call(
        functools.partial(own_kernel, block_width),
        [WHOLE] * 3,
        [((rows, pair_width), jnp.bfloat16)],
        16 * MIB,
        block_flops * pair_width,
    )(attended, weight, in_vmem(residual))

    def projected(*groups):
        return local_call(
            functools.partial(project_kernel, groups, block_width),
            [WHOLE] * 2,
            [((len(xs), rows, width), jnp.bfloat16) for xs, _, width in groups],
            16 * MIB,
            block_flops * sum(len(xs) * width for xs, _, width in groups),
        )(attended, weight)

    half = n_tp // 2
    own_a = handed(own_a, 0)
    send_b, pair_a = projected((list(range(half, n_tp)), pair_width, cross_width), ([1], 0, pair_width))
    kept_a, kept_b = projected((across, 0, pair_width), (list(range(half)), pair_width, cross_width))
    got_a = exchange(send_a, "tp", 1)
    got_b = exchange(send_b, "tp", half)
    pair_a = handed(pair_a[0], 1)

    part = [kept_a[i].astype(jnp.float32) + got_a[i].astype(jnp.float32) for i in range(len(across))]
    own_a, *part = lax.optimization_barrier((own_a, *[a.astype(jnp.bfloat16) for a in part]))
    terms_a = [own_a, pair_a]
    bit = 2
    while bit < n_tp:
        count = (len(part) + 1) // 2
        sends = part[:count]
        received = [exchange(a, "tp", bit) for a in sends[:-1]]
        terms_a.append(handed(sends[-1], bit))
        part = [(a.astype(jnp.float32) + r.astype(jnp.float32)).astype(jnp.bfloat16) for a, r in zip(part[count:], received)]
        bit *= 2

    part = [kept_b[i].astype(jnp.float32) + got_b[i].astype(jnp.float32) for i in range(half)]
    while len(part) > 2:
        count = len(part) // 2
        received = [exchange(a.astype(jnp.bfloat16), "tp", count) for a in part[count:]]
        part = [a + r.astype(jnp.float32) for a, r in zip(part[:count], received)]
    part[0] = part[0] + residual[0, :, pair_width:].astype(jnp.float32)
    part = [a.astype(jnp.bfloat16) for a in part]
    terms_b = [handed(a, x) for x, a in enumerate(part)]

    terms = [*terms_a, *terms_b]
    (out,) = pl.pallas_call(
        functools.partial(total_kernel, len(terms_a)),
        in_specs=[WHOLE] * len(terms),
        out_shape=[pltpu.HBM((rows, block_width), jnp.bfloat16)],
        out_specs=[IN_HBM],
        scratch_shapes=[pltpu.VMEM((rows, block_width), jnp.bfloat16), pltpu.SemaphoreType.DMA((2,))],
        compiler_params=pltpu.CompilerParams(vmem_limit_bytes=16 * MIB),
    )(*[in_vmem(term) for term in terms])
    return out[None]


def solution(mesh):
    placed = (
        P("section"),
        P("section", "ctx", "tp"),
        P("section", "ctx", "tp"),
        P("section", "ctx", "tp"),
        P("section", "ctx", "tp"),
        P("section", "tp", None),
    )
    return jax.shard_map(
        on_device, mesh=mesh, in_specs=placed, out_specs=P("section", "ctx", "tp"), check_vma=False
    )
```

```python
import functools
import math

import jax
import jax.numpy as jnp
from jax import lax
from jax.experimental import pallas as pl
from jax.experimental.pallas import tpu as pltpu
from jax.sharding import PartitionSpec as P

HD = 128
G = 4
LANES = 128
NEG_FILL = -1e30
MAX_FLOOR = -1e29
EXP_SCALE = HD ** (-0.5) * math.log2(math.e)
LOG2_E = math.log2(math.e)
LOG_ROWS = 8
LOG_SPACE = 32
MIB = 1 << 20

WHOLE = pl.BlockSpec(memory_space=pltpu.VMEM)
IN_HBM = pl.BlockSpec(memory_space=pltpu.HBM)
SCALARS = pl.BlockSpec(memory_space=pltpu.SMEM)


def exchange(block, axis, mask):
    route = [(i, i ^ mask) for i in range(lax.axis_size(axis))]
    return lax.ppermute(block, axis, route)


def handed(block, mask):
    sections, n_tp = lax.axis_size("section"), lax.axis_size("tp")
    route = [(s * n_tp + i, (s + 1) % sections * n_tp + (i ^ mask)) for s in range(sections) for i in range(n_tp)]
    return lax.ppermute(block, ("section", "tp"), route)


def in_vmem(array):
    return pltpu.with_memory_space_constraint(array, pltpu.VMEM)


def local_call(body, ins, outs, limit, flops, scratch=()):
    return pl.pallas_call(
        body,
        in_specs=ins,
        out_shape=[pltpu.VMEM(shape, dtype) for shape, dtype in outs],
        out_specs=[WHOLE] * len(outs),
        scratch_shapes=list(scratch),
        compiler_params=pltpu.CompilerParams(vmem_limit_bytes=limit),
        cost_estimate=pl.CostEstimate(flops=flops, bytes_accessed=0, transcendentals=0),
    )


def stacked_query(q_ref, kv_head):
    heads = range(kv_head * G, (kv_head + 1) * G)
    return jnp.concatenate([q_ref[0, :, h * HD : (h + 1) * HD] for h in heads], axis=0)


def masked_scores(query, key_ref, kv_head, bound):
    keys = key_ref[0, :, kv_head * HD : (kv_head + 1) * HD]
    scores = lax.dot_general(query, keys, (((1,), (1,)), ((), ())), preferred_element_type=jnp.float32)
    rows = query.shape[0] // G
    ahead = lax.broadcasted_iota(jnp.int32, scores.shape, 1) - lax.broadcasted_iota(jnp.int32, scores.shape, 0) % rows
    return jnp.where(ahead <= bound, scores, NEG_FILL)


def attend(query, key_refs, value_refs, kv_head, bounds):
    columns = slice(kv_head * HD, (kv_head + 1) * HD)
    parts = [masked_scores(query, ref, kv_head, bound) for ref, bound in zip(key_refs, bounds)]
    top = functools.reduce(jnp.maximum, [jnp.max(part, axis=1, keepdims=True) for part in parts])
    top = jnp.maximum(top, MAX_FLOOR)
    weights = [jnp.exp2((part - top) * EXP_SCALE) for part in parts]
    total = sum(jnp.sum(part, axis=1, keepdims=True) for part in weights)
    mixed = sum(
        jnp.dot(part.astype(jnp.bfloat16), ref[0, :, columns], preferred_element_type=jnp.float32)
        for part, ref in zip(weights, value_refs)
    )
    some = total > 0.0
    total = jnp.where(some, total, 1.0)
    return mixed / total, jnp.where(some, top * EXP_SCALE + jnp.log(total) * LOG2_E, NEG_FILL)


def copy_all(pairs, sems):
    copies = [pltpu.make_async_copy(source, target, sems.at[i]) for i, (source, target) in enumerate(pairs)]
    for copy in copies:
        copy.start()
    return copies


def query_kernel(q_hbm, *refs):
    *query_refs, q_ref, sem = refs
    copy = pltpu.make_async_copy(q_hbm, q_ref, sem)
    copy.start()
    copy.wait()
    for kv_head, query_ref in enumerate(query_refs):
        query_ref[...] = stacked_query(q_ref, kv_head)


def cache_kernel(key_hbm, value_hbm, w_hbm, key_ref, value_ref, w_ref, sems):
    span = pl.ds(0, w_ref.shape[1])
    for copy in copy_all(((key_hbm, key_ref), (value_hbm, value_ref), (w_hbm.at[:, span], w_ref)), sems):
        copy.wait()


def bounds_of(masks, offset, block, rows, length):
    own = lax.axis_index("ctx")
    return [offset + block * rows - (own ^ mask) * length for mask in masks]


def near_kernel(masks, kv_local, offset_ref, w_hbm, *refs):
    count = len(masks)
    query_refs, refs = refs[:kv_local], refs[kv_local:]
    key_refs, value_refs, refs = refs[:count], refs[count : 2 * count], refs[2 * count :]
    result_ref, log_ref, *w_refs, sems = refs
    heights = [ref.shape[1] for ref in w_refs]
    parts = [w_hbm.at[:, pl.ds((i + 1) * height, height)] for i, height in enumerate(heights)]
    copies = copy_all(zip(parts, w_refs), sems)
    rows, length = query_refs[0].shape[0] // G, key_refs[0].shape[1]
    bounds = bounds_of(masks, offset_ref[0], lax.axis_index("ctx"), rows, length)
    for kv_head, query_ref in enumerate(query_refs):
        result, log_sum = attend(query_ref[...], key_refs, value_refs, kv_head, bounds)
        result_ref[kv_head] = result
        log_ref[kv_head] = jnp.broadcast_to(log_sum, log_ref.shape[1:])
    for copy in copies:
        copy.wait()


def far_kernel(masks, far, kv_head, offset_ref, query_ref, *refs):
    count = len(masks)
    key_refs, value_refs, (out_ref,) = refs[:count], refs[count : 2 * count], refs[2 * count :]
    stacked = query_ref.shape[0]
    rows, length = stacked // G, key_refs[0].shape[1]
    bounds = bounds_of(masks, offset_ref[0], lax.axis_index("ctx") ^ far, rows, length)
    result, log_sum = attend(query_ref[...], key_refs, value_refs, kv_head, bounds)
    out_ref[:stacked] = result.astype(jnp.bfloat16)
    lane = lax.broadcasted_iota(jnp.int32, (rows, LANES), 1)
    logs = jnp.zeros((rows, LANES), jnp.float32)
    for g in range(G):
        logs = jnp.where(lane == g, log_sum[g * rows : (g + 1) * rows], logs)
    logs = logs.T[:LOG_ROWS]
    high = logs.astype(jnp.bfloat16).astype(jnp.float32)
    middle = (logs - high).astype(jnp.bfloat16).astype(jnp.float32)
    low = logs - high - middle
    rest = jnp.zeros((LOG_SPACE - 3 * LOG_ROWS, rows), jnp.float32)
    out_ref[stacked:] = jnp.concatenate([high, middle, low, rest], axis=0).astype(jnp.bfloat16)


def block_columns(group, slot, block_width):
    xs, lower, width = group
    return pl.ds(pl.multiple_of((lax.axis_index("tp") ^ xs[slot]) * block_width + lower, LANES), width)


def projected_block(att_refs, w_refs, columns):
    return sum(
        jnp.dot(att_ref[...], w_ref[0, :, columns], preferred_element_type=jnp.float32)
        for att_ref, w_ref in zip(att_refs, w_refs)
    )


def combine_kernel(kv_head, group, block_width, near_ref, log_ref, far_ref, w_ref, *refs):
    *before_refs, att_ref, send_ref = refs
    rows = att_ref.shape[0]
    stacked = G * rows
    parts = far_ref[stacked:].astype(jnp.float32)
    logs = sum(parts[i * LOG_ROWS : (i + 1) * LOG_ROWS] for i in range(3))
    logs = jnp.concatenate([logs, jnp.zeros((LANES - LOG_ROWS, rows), jnp.float32)], axis=0).T
    for g in range(G):
        span = slice(g * rows, (g + 1) * rows)
        near_log, far_log = log_ref[kv_head, span, :1], logs[:, g : g + 1]
        top = jnp.maximum(near_log, far_log)
        near_weight, far_weight = jnp.exp2(near_log - top), jnp.exp2(far_log - top)
        scale = 1.0 / (near_weight + far_weight)
        mixed = near_ref[kv_head, span] * (near_weight * scale)
        mixed += far_ref[span].astype(jnp.float32) * (far_weight * scale)
        att_ref[:, g * HD : (g + 1) * HD] = mixed.astype(jnp.bfloat16)
    for slot in range(len(group[0])):
        block = projected_block([att_ref], [w_ref], block_columns(group, slot, block_width))
        for before_ref in before_refs:
            block += before_ref[slot]
        send_ref[slot] = block.astype(send_ref.dtype)


def own_kernel(count, group, block_width, *refs):
    att_refs, w_refs, (residual_ref, own_ref) = refs[:count], refs[count : 2 * count], refs[2 * count :]
    own = projected_block(att_refs, w_refs, block_columns(group, 0, block_width))
    own_ref[...] = (residual_ref[0, :, : own_ref.shape[1]].astype(jnp.float32) + own).astype(jnp.bfloat16)


def project_kernel(count, groups, block_width, *refs):
    att_refs, w_refs, out_refs = refs[:count], refs[count : 2 * count], refs[2 * count :]
    for group, out_ref in zip(groups, out_refs):
        for slot in range(len(group[0])):
            block = projected_block(att_refs, w_refs, block_columns(group, slot, block_width))
            out_ref[slot] = block.astype(jnp.bfloat16)


def total_kernel(count, *refs):
    *term_refs, out_ref, total_ref, sems = refs
    lower = term_refs[0].shape[1]
    half = out_ref.shape[0] // 2
    copies = []
    for i, rows in enumerate((slice(0, half), slice(half, 2 * half))):
        for group, columns in ((term_refs[:count], slice(0, lower)), (term_refs[count:], slice(lower, None))):
            total_ref[rows, columns] = sum(ref[rows].astype(jnp.float32) for ref in group).astype(jnp.bfloat16)
        copies.append(pltpu.make_async_copy(total_ref.at[rows], out_ref.at[rows], sems.at[i]))
        copies[-1].start()
    for copy in copies:
        copy.wait()


def xor_order(lowest, size):
    if lowest >= size:
        return [0]
    rest = xor_order(lowest * 2, size)
    return [x + lowest for x in rest] + rest


def cross_first_width(width):
    return max(1, (2 * (width // LANES)) // 10) * LANES


def on_device(row_offsets, queries, cache_keys, cache_values, residual, out_weight):
    n_ctx, n_tp = lax.axis_size("ctx"), lax.axis_size("tp")
    rows = queries.shape[1]
    kv_local = cache_keys.shape[2] // HD
    stacked = G * rows
    top_bit = n_ctx // 2
    block_width = out_weight.shape[2] // n_tp
    bf16, f32 = jnp.bfloat16, jnp.float32

    in_hbm = [pltpu.with_memory_space_constraint(a, pltpu.HBM) for a in (queries, cache_keys, cache_values, out_weight)]
    own_queries = local_call(
        query_kernel,
        [IN_HBM],
        [((stacked, HD), bf16)] * kv_local,
        16 * MIB,
        0,
        [pltpu.VMEM(queries.shape, bf16), pltpu.SemaphoreType.DMA],
    )(in_hbm[0])
    far_queries = [exchange(query, "ctx", top_bit) for query in own_queries]
    near = [(0, cache_keys, cache_values)]
    bit = top_bit // 2
    while bit:
        near += [(m | bit, exchange(k, "ctx", bit), exchange(v, "ctx", bit)) for m, k, v in near]
        bit //= 2
    w_shape = (1, G * HD, out_weight.shape[2])
    own_keys, own_values, first_weight = local_call(
        cache_kernel,
        [IN_HBM] * 3,
        [(cache_keys.shape, bf16), (cache_values.shape, bf16), (w_shape, bf16)],
        16 * MIB,
        0,
        [pltpu.SemaphoreType.DMA((3,))],
    )(*in_hbm[1:])
    masks, near_keys, near_values = zip(*near)
    cached = [in_vmem(a) for a in (own_keys, *near_keys[1:], own_values, *near_values[1:])]
    far_results = []
    for kv_head in range(kv_local):
        query = far_queries[kv_head]
        if kv_head:
            query, _ = lax.optimization_barrier((query, result))
        (result,) = local_call(
            functools.partial(far_kernel, masks, top_bit, kv_head),
            [SCALARS] + [WHOLE] * (1 + len(cached)),
            [((stacked + LOG_SPACE, HD), bf16)],
            24 * MIB,
            0,
        )(row_offsets, in_vmem(query), *cached)
        far_results.append(exchange(result, "ctx", top_bit))
    near_result, near_log, *weights = local_call(
        functools.partial(near_kernel, masks, kv_local),
        [SCALARS, IN_HBM] + [WHOLE] * (kv_local + len(cached)),
        [((kv_local, stacked, HD), f32)] * 2 + [(w_shape, bf16)] * (kv_local - 1),
        24 * MIB,
        0,
        [pltpu.SemaphoreType.DMA((kv_local,))],
    )(row_offsets, in_hbm[3], *own_queries, *cached)
    weights = [first_weight, *weights]

    across = xor_order(2, n_tp)[:-1]
    cross_width = cross_first_width(block_width)
    pair_width = block_width - cross_width
    block_flops = 2 * rows * out_weight.shape[1]
    relay = ([1 ^ x for x in across], 0, pair_width)
    attended, sent = [], []
    for kv_head, result in enumerate(far_results):
        kind = bf16 if kv_head + 1 == kv_local else f32
        head, *sent = local_call(
            functools.partial(combine_kernel, kv_head, relay, block_width),
            [WHOLE] * (4 + len(sent)),
            [((rows, G * HD), bf16), ((len(across), rows, pair_width), kind)],
            24 * MIB,
            0,
        )(near_result, near_log, in_vmem(result), weights[kv_head], *sent)
        attended.append(head)
    (send_a,) = sent
    (own_a,) = local_call(
        functools.partial(own_kernel, kv_local, ([0], 0, pair_width), block_width),
        [WHOLE] * (2 * kv_local + 1),
        [((rows, pair_width), bf16)],
        16 * MIB,
        block_flops * pair_width,
    )(*attended, *weights, in_vmem(residual))

    def projected(*groups):
        return local_call(
            functools.partial(project_kernel, kv_local, groups, block_width),
            [WHOLE] * (2 * kv_local),
            [((len(xs), rows, width), bf16) for xs, _, width in groups],
            16 * MIB,
            block_flops * sum(len(xs) * width for xs, _, width in groups),
        )(*attended, *weights)

    half = n_tp // 2
    own_a = handed(own_a, 0)
    send_b, pair_a = projected((list(range(half, n_tp)), pair_width, cross_width), ([1], 0, pair_width))
    kept_a, kept_b = projected((across, 0, pair_width), (list(range(half)), pair_width, cross_width))
    got_a = exchange(send_a, "tp", 1)
    got_b = exchange(send_b, "tp", half)
    pair_a = handed(pair_a[0], 1)

    part = [kept_a[i].astype(jnp.float32) + got_a[i].astype(jnp.float32) for i in range(len(across))]
    own_a, *part = lax.optimization_barrier((own_a, *[a.astype(jnp.bfloat16) for a in part]))
    terms_a = [own_a, pair_a]
    bit = 2
    while bit < n_tp:
        count = (len(part) + 1) // 2
        sends = part[:count]
        received = [exchange(a, "tp", bit) for a in sends[:-1]]
        terms_a.append(handed(sends[-1], bit))
        part = [(a.astype(jnp.float32) + r.astype(jnp.float32)).astype(jnp.bfloat16) for a, r in zip(part[count:], received)]
        bit *= 2

    part = [kept_b[i].astype(jnp.float32) + got_b[i].astype(jnp.float32) for i in range(half)]
    while len(part) > 2:
        count = len(part) // 2
        received = [exchange(a.astype(jnp.bfloat16), "tp", count) for a in part[count:]]
        part = [a + r.astype(jnp.float32) for a, r in zip(part[:count], received)]
    part[0] = part[0] + residual[0, :, pair_width:].astype(jnp.float32)
    part = [a.astype(jnp.bfloat16) for a in part]
    terms_b = [handed(a, x) for x, a in enumerate(part)]

    terms = [*terms_a, *terms_b]
    (out,) = pl.pallas_call(
        functools.partial(total_kernel, len(terms_a)),
        in_specs=[WHOLE] * len(terms),
        out_shape=[pltpu.HBM((rows, block_width), jnp.bfloat16)],
        out_specs=[IN_HBM],
        scratch_shapes=[pltpu.VMEM((rows, block_width), jnp.bfloat16), pltpu.SemaphoreType.DMA((2,))],
        compiler_params=pltpu.CompilerParams(vmem_limit_bytes=16 * MIB),
    )(*[in_vmem(term) for term in terms])
    return out[None]


def solution(mesh):
    placed = (
        P("section"),
        P("section", "ctx", "tp"),
        P("section", "ctx", "tp"),
        P("section", "ctx", "tp"),
        P("section", "ctx", "tp"),
        P("section", "tp", None),
    )
    return jax.shard_map(
        on_device, mesh=mesh, in_specs=placed, out_specs=P("section", "ctx", "tp"), check_vma=False
    )
```

```python
import functools
import math

import jax
import jax.numpy as jnp
from jax import lax
from jax.experimental import pallas as pl
from jax.experimental.pallas import tpu as pltpu
from jax.sharding import PartitionSpec as P

HD = 128
G = 4
LANES = 128
NEG_FILL = -1e30
MAX_FLOOR = -1e29
EXP_SCALE = HD ** (-0.5) * math.log2(math.e)
LOG2_E = math.log2(math.e)
LOG_ROWS = G
LOG_SPACE = 16
MIB = 1 << 20

WHOLE = pl.BlockSpec(memory_space=pltpu.VMEM)
IN_HBM = pl.BlockSpec(memory_space=pltpu.HBM)
SCALARS = pl.BlockSpec(memory_space=pltpu.SMEM)


def exchange(block, axis, mask):
    route = [(i, i ^ mask) for i in range(lax.axis_size(axis))]
    return lax.ppermute(block, axis, route)


def handed(block, mask):
    sections, n_tp = lax.axis_size("section"), lax.axis_size("tp")
    route = [(s * n_tp + i, (s + 1) % sections * n_tp + (i ^ mask)) for s in range(sections) for i in range(n_tp)]
    return lax.ppermute(block, ("section", "tp"), route)


def in_vmem(array):
    return pltpu.with_memory_space_constraint(array, pltpu.VMEM)


def local_call(body, ins, outs, limit, flops, scratch=()):
    return pl.pallas_call(
        body,
        in_specs=ins,
        out_shape=[pltpu.VMEM(shape, dtype) for shape, dtype in outs],
        out_specs=[WHOLE] * len(outs),
        scratch_shapes=list(scratch),
        compiler_params=pltpu.CompilerParams(vmem_limit_bytes=limit),
        cost_estimate=pl.CostEstimate(flops=flops, bytes_accessed=0, transcendentals=0),
    )


def stacked_query(q_ref, kv_head):
    heads = range(kv_head * G, (kv_head + 1) * G)
    return jnp.concatenate([q_ref[0, :, h * HD : (h + 1) * HD] for h in heads], axis=0)


def masked_scores(query, key_ref, kv_head, bound):
    keys = key_ref[0, :, kv_head * HD : (kv_head + 1) * HD]
    scores = lax.dot_general(query, keys, (((1,), (1,)), ((), ())), preferred_element_type=jnp.float32)
    stacked, length = scores.shape
    row = lax.rem(lax.broadcasted_iota(jnp.int32, (stacked, 1), 0), jnp.int32(stacked // G))
    visible = lax.broadcasted_iota(jnp.int32, (1, length), 1) <= row + bound
    return jnp.where(visible, scores, NEG_FILL)


def attend(query, key_refs, value_refs, kv_head, bounds):
    columns = slice(kv_head * HD, (kv_head + 1) * HD)
    parts = [masked_scores(query, ref, kv_head, bound) for ref, bound in zip(key_refs, bounds)]
    top = functools.reduce(jnp.maximum, [jnp.max(part, axis=1, keepdims=True) for part in parts])
    top = jnp.maximum(top, MAX_FLOOR)
    weights = [jnp.exp2((part - top) * EXP_SCALE) for part in parts]
    total = sum(jnp.sum(part, axis=1, keepdims=True) for part in weights)
    mixed = sum(
        jnp.dot(part.astype(jnp.bfloat16), ref[0, :, columns], preferred_element_type=jnp.float32)
        for part, ref in zip(weights, value_refs)
    )
    some = total > 0.0
    total = jnp.where(some, total, 1.0)
    return mixed / total, jnp.where(some, top * EXP_SCALE + jnp.log(total) * LOG2_E, NEG_FILL)


def copy_all(pairs, sems):
    copies = [pltpu.make_async_copy(source, target, sems.at[i]) for i, (source, target) in enumerate(pairs)]
    for copy in copies:
        copy.start()
    return copies


def query_kernel(q_hbm, *refs):
    *query_refs, sems = refs
    rows = q_hbm.shape[1]
    heads = [(query_ref, g) for query_ref in query_refs for g in range(G)]
    parts = [(q_hbm.at[0, :, pl.ds(h * HD, HD)], ref.at[pl.ds(g * rows, rows)]) for h, (ref, g) in enumerate(heads)]
    for copy in copy_all(parts, sems):
        copy.wait()


def cache_kernel(key_hbm, value_hbm, w_hbm, key_ref, value_ref, w_ref, sems):
    span = pl.ds(0, w_ref.shape[1])
    for copy in copy_all(((key_hbm, key_ref), (value_hbm, value_ref), (w_hbm.at[:, span], w_ref)), sems):
        copy.wait()


def bounds_of(masks, offset, block, rows, length):
    own = lax.axis_index("ctx")
    return [offset + block * rows - (own ^ mask) * length for mask in masks]


def near_kernel(masks, kv_local, offset_ref, w_hbm, *refs):
    count = len(masks)
    query_refs, refs = refs[:kv_local], refs[kv_local:]
    key_refs, value_refs, refs = refs[:count], refs[count : 2 * count], refs[2 * count :]
    result_ref, log_ref, *w_refs, sems = refs
    heights = [ref.shape[1] for ref in w_refs]
    parts = [w_hbm.at[:, pl.ds((i + 1) * height, height)] for i, height in enumerate(heights)]
    copies = copy_all(zip(parts, w_refs), sems)
    rows, length = query_refs[0].shape[0] // G, key_refs[0].shape[1]
    bounds = bounds_of(masks, offset_ref[0], lax.axis_index("ctx"), rows, length)
    for kv_head, query_ref in enumerate(query_refs):
        result, log_sum = attend(query_ref[...], key_refs, value_refs, kv_head, bounds)
        result_ref[kv_head] = result
        log_ref[kv_head] = jnp.broadcast_to(log_sum, log_ref.shape[1:])
    for copy in copies:
        copy.wait()


def far_kernel(masks, far, kv_head, offset_ref, query_ref, *refs):
    count = len(masks)
    key_refs, value_refs, (out_ref,) = refs[:count], refs[count : 2 * count], refs[2 * count :]
    stacked = query_ref.shape[0]
    rows, length = stacked // G, key_refs[0].shape[1]
    bounds = bounds_of(masks, offset_ref[0], lax.axis_index("ctx") ^ far, rows, length)
    result, log_sum = attend(query_ref[...], key_refs, value_refs, kv_head, bounds)
    out_ref[:stacked] = result.astype(jnp.bfloat16)
    lane = lax.broadcasted_iota(jnp.int32, (rows, LANES), 1)
    logs = jnp.zeros((rows, LANES), jnp.float32)
    for g in range(G):
        logs = jnp.where(lane == g, log_sum[g * rows : (g + 1) * rows], logs)
    logs = logs.T[:LOG_ROWS]
    high = logs.astype(jnp.bfloat16).astype(jnp.float32)
    middle = (logs - high).astype(jnp.bfloat16).astype(jnp.float32)
    low = logs - high - middle
    rest = jnp.zeros((LOG_SPACE - 3 * LOG_ROWS, rows), jnp.float32)
    out_ref[stacked:] = jnp.concatenate([high, middle, low, rest], axis=0).astype(jnp.bfloat16)


def block_columns(group, slot, block_width):
    xs, lower, width = group
    return pl.ds(pl.multiple_of((lax.axis_index("tp") ^ xs[slot]) * block_width + lower, LANES), width)


def projected_block(att_refs, w_refs, columns):
    return sum(
        jnp.dot(att_ref[...], w_ref[0, :, columns], preferred_element_type=jnp.float32)
        for att_ref, w_ref in zip(att_refs, w_refs)
    )


def combine_kernel(kv_head, group, block_width, near_ref, log_ref, far_ref, w_ref, *refs):
    *before_refs, att_ref, send_ref = refs
    rows = att_ref.shape[0]
    stacked = G * rows
    parts = far_ref[stacked:].astype(jnp.float32)
    logs = sum(parts[i * LOG_ROWS : (i + 1) * LOG_ROWS] for i in range(3))
    logs = jnp.concatenate([logs, jnp.zeros((LANES - LOG_ROWS, rows), jnp.float32)], axis=0).T
    for g in range(G):
        span = slice(g * rows, (g + 1) * rows)
        near_log, far_log = log_ref[kv_head, span, :1], logs[:, g : g + 1]
        top = jnp.maximum(near_log, far_log)
        near_weight, far_weight = jnp.exp2(near_log - top), jnp.exp2(far_log - top)
        scale = 1.0 / (near_weight + far_weight)
        mixed = near_ref[kv_head, span] * (near_weight * scale)
        mixed += far_ref[span].astype(jnp.float32) * (far_weight * scale)
        att_ref[:, g * HD : (g + 1) * HD] = mixed.astype(jnp.bfloat16)
    for slot in range(len(group[0])):
        block = projected_block([att_ref], [w_ref], block_columns(group, slot, block_width))
        for before_ref in before_refs:
            block += before_ref[slot]
        send_ref[slot] = block.astype(send_ref.dtype)


def own_kernel(count, group, block_width, *refs):
    att_refs, w_refs, (residual_ref, own_ref) = refs[:count], refs[count : 2 * count], refs[2 * count :]
    own = projected_block(att_refs, w_refs, block_columns(group, 0, block_width))
    own_ref[...] = (residual_ref[0, :, : own_ref.shape[1]].astype(jnp.float32) + own).astype(jnp.bfloat16)


def project_kernel(count, groups, block_width, *refs):
    att_refs, w_refs, out_refs = refs[:count], refs[count : 2 * count], refs[2 * count :]
    for group, out_ref in zip(groups, out_refs):
        for slot in range(len(group[0])):
            block = projected_block(att_refs, w_refs, block_columns(group, slot, block_width))
            out_ref[slot] = block.astype(jnp.bfloat16)


def total_kernel(count, *refs):
    *term_refs, out_ref, total_ref, sems = refs
    lower = term_refs[0].shape[1]
    half = out_ref.shape[0] // 2
    copies = []
    for i, rows in enumerate((slice(0, half), slice(half, 2 * half))):
        for group, columns in ((term_refs[:count], slice(0, lower)), (term_refs[count:], slice(lower, None))):
            total_ref[rows, columns] = sum(ref[rows].astype(jnp.float32) for ref in group).astype(jnp.bfloat16)
        copies.append(pltpu.make_async_copy(total_ref.at[rows], out_ref.at[rows], sems.at[i]))
        copies[-1].start()
    for copy in copies:
        copy.wait()


def xor_order(lowest, size):
    if lowest >= size:
        return [0]
    rest = xor_order(lowest * 2, size)
    return [x + lowest for x in rest] + rest


def cross_first_width(width):
    return max(1, (2 * (width // LANES)) // 10) * LANES


def on_device(row_offsets, queries, cache_keys, cache_values, residual, out_weight):
    n_ctx, n_tp = lax.axis_size("ctx"), lax.axis_size("tp")
    rows = queries.shape[1]
    kv_local = cache_keys.shape[2] // HD
    stacked = G * rows
    top_bit = n_ctx // 2
    block_width = out_weight.shape[2] // n_tp
    bf16, f32 = jnp.bfloat16, jnp.float32

    in_hbm = [pltpu.with_memory_space_constraint(a, pltpu.HBM) for a in (queries, cache_keys, cache_values, out_weight)]
    own_queries = local_call(
        query_kernel,
        [IN_HBM],
        [((stacked, HD), bf16)] * kv_local,
        16 * MIB,
        0,
        [pltpu.SemaphoreType.DMA((kv_local * G,))],
    )(in_hbm[0])
    near = [(0, cache_keys, cache_values)]
    bit = top_bit // 2
    while bit:
        near += [(m | bit, exchange(k, "ctx", bit), exchange(v, "ctx", bit)) for m, k, v in near]
        bit //= 2
    w_shape = (1, G * HD, out_weight.shape[2])
    own_keys, own_values, first_weight = local_call(
        cache_kernel,
        [IN_HBM] * 3,
        [(cache_keys.shape, bf16), (cache_values.shape, bf16), (w_shape, bf16)],
        16 * MIB,
        0,
        [pltpu.SemaphoreType.DMA((3,))],
    )(*in_hbm[1:])
    sent_queries = list(own_queries)
    sent_queries[1:], first_weight = lax.optimization_barrier((sent_queries[1:], first_weight))
    far_queries = [exchange(query, "ctx", top_bit) for query in sent_queries]
    masks, near_keys, near_values = zip(*near)
    cached = [in_vmem(a) for a in (own_keys, *near_keys[1:], own_values, *near_values[1:])]
    far_results = []
    for kv_head in range(kv_local):
        query = far_queries[kv_head]
        if kv_head:
            query, _ = lax.optimization_barrier((query, result))
        (result,) = local_call(
            functools.partial(far_kernel, masks, top_bit, kv_head),
            [SCALARS] + [WHOLE] * (1 + len(cached)),
            [((stacked + LOG_SPACE, HD), bf16)],
            24 * MIB,
            0,
        )(row_offsets, in_vmem(query), *cached)
        far_results.append(exchange(result, "ctx", top_bit))
    near_result, near_log, *weights = local_call(
        functools.partial(near_kernel, masks, kv_local),
        [SCALARS, IN_HBM] + [WHOLE] * (kv_local + len(cached)),
        [((kv_local, stacked, HD), f32)] * 2 + [(w_shape, bf16)] * (kv_local - 1),
        24 * MIB,
        0,
        [pltpu.SemaphoreType.DMA((kv_local,))],
    )(row_offsets, in_hbm[3], *own_queries, *cached)
    weights = [first_weight, *weights]

    across = xor_order(2, n_tp)[:-1]
    cross_width = cross_first_width(block_width)
    pair_width = block_width - cross_width
    block_flops = 2 * rows * out_weight.shape[1]
    relay = ([1 ^ x for x in across], 0, pair_width)
    attended, sent = [], []
    for kv_head, result in enumerate(far_results):
        kind = bf16 if kv_head + 1 == kv_local else f32
        head, *sent = local_call(
            functools.partial(combine_kernel, kv_head, relay, block_width),
            [WHOLE] * (4 + len(sent)),
            [((rows, G * HD), bf16), ((len(across), rows, pair_width), kind)],
            24 * MIB,
            0,
        )(near_result, near_log, in_vmem(result), weights[kv_head], *sent)
        attended.append(head)
    (send_a,) = sent
    (own_a,) = local_call(
        functools.partial(own_kernel, kv_local, ([0], 0, pair_width), block_width),
        [WHOLE] * (2 * kv_local + 1),
        [((rows, pair_width), bf16)],
        16 * MIB,
        block_flops * pair_width,
    )(*attended, *weights, in_vmem(residual))

    def projected(*groups):
        return local_call(
            functools.partial(project_kernel, kv_local, groups, block_width),
            [WHOLE] * (2 * kv_local),
            [((len(xs), rows, width), bf16) for xs, _, width in groups],
            16 * MIB,
            block_flops * sum(len(xs) * width for xs, _, width in groups),
        )(*attended, *weights)

    half = n_tp // 2
    own_a = handed(own_a, 0)
    send_b, pair_a = projected((list(range(half, n_tp)), pair_width, cross_width), ([1], 0, pair_width))
    kept_a, kept_b = projected((across, 0, pair_width), (list(range(half)), pair_width, cross_width))
    got_a = exchange(send_a, "tp", 1)
    got_b = exchange(send_b, "tp", half)
    pair_a = handed(pair_a[0], 1)

    part = [kept_a[i].astype(jnp.float32) + got_a[i].astype(jnp.float32) for i in range(len(across))]
    own_a, *part = lax.optimization_barrier((own_a, *[a.astype(jnp.bfloat16) for a in part]))
    terms_a = [own_a, pair_a]
    bit = 2
    while bit < n_tp:
        count = (len(part) + 1) // 2
        sends = part[:count]
        received = [exchange(a, "tp", bit) for a in sends[:-1]]
        terms_a.append(handed(sends[-1], bit))
        part = [(a.astype(jnp.float32) + r.astype(jnp.float32)).astype(jnp.bfloat16) for a, r in zip(part[count:], received)]
        bit *= 2

    part = [kept_b[i].astype(jnp.float32) + got_b[i].astype(jnp.float32) for i in range(half)]
    while len(part) > 2:
        count = len(part) // 2
        received = [exchange(a.astype(jnp.bfloat16), "tp", count) for a in part[count:]]
        part = [a + r.astype(jnp.float32) for a, r in zip(part[:count], received)]
    part[0] = part[0] + residual[0, :, pair_width:].astype(jnp.float32)
    part = [a.astype(jnp.bfloat16) for a in part]
    terms_b = [handed(a, x) for x, a in enumerate(part)]

    terms = [*terms_a, *terms_b]
    (out,) = pl.pallas_call(
        functools.partial(total_kernel, len(terms_a)),
        in_specs=[WHOLE] * len(terms),
        out_shape=[pltpu.HBM((rows, block_width), jnp.bfloat16)],
        out_specs=[IN_HBM],
        scratch_shapes=[pltpu.VMEM((rows, block_width), jnp.bfloat16), pltpu.SemaphoreType.DMA((2,))],
        compiler_params=pltpu.CompilerParams(vmem_limit_bytes=16 * MIB),
    )(*[in_vmem(term) for term in terms])
    return out[None]


def solution(mesh):
    placed = (
        P("section"),
        P("section", "ctx", "tp"),
        P("section", "ctx", "tp"),
        P("section", "ctx", "tp"),
        P("section", "ctx", "tp"),
        P("section", "tp", None),
    )
    return jax.shard_map(
        on_device, mesh=mesh, in_specs=placed, out_specs=P("section", "ctx", "tp"), check_vma=False
    )
```

```python
import functools
import math

import jax
import jax.numpy as jnp
from jax import lax
from jax.experimental import pallas as pl
from jax.experimental.pallas import tpu as pltpu
from jax.sharding import PartitionSpec as P

HD = 128
G = 4
LANES = 128
NEG_FILL = -1e30
MAX_FLOOR = -1e29
EXP_SCALE = HD ** (-0.5) * math.log2(math.e)
LOG2_E = math.log2(math.e)
LOG_ROWS = G
LOG_SPACE = 16
MIB = 1 << 20

WHOLE = pl.BlockSpec(memory_space=pltpu.VMEM)
IN_HBM = pl.BlockSpec(memory_space=pltpu.HBM)
SCALARS = pl.BlockSpec(memory_space=pltpu.SMEM)


def exchange(block, axis, mask):
    route = [(i, i ^ mask) for i in range(lax.axis_size(axis))]
    return lax.ppermute(block, axis, route)


def handed(block, mask):
    sections, n_tp = lax.axis_size("section"), lax.axis_size("tp")
    route = [(s * n_tp + i, (s + 1) % sections * n_tp + (i ^ mask)) for s in range(sections) for i in range(n_tp)]
    return lax.ppermute(block, ("section", "tp"), route)


def in_vmem(array):
    return pltpu.with_memory_space_constraint(array, pltpu.VMEM)


def local_call(body, ins, outs, limit, flops, scratch=()):
    return pl.pallas_call(
        body,
        in_specs=ins,
        out_shape=[pltpu.VMEM(shape, dtype) for shape, dtype in outs],
        out_specs=[WHOLE] * len(outs),
        scratch_shapes=list(scratch),
        compiler_params=pltpu.CompilerParams(vmem_limit_bytes=limit),
        cost_estimate=pl.CostEstimate(flops=flops, bytes_accessed=0, transcendentals=0),
    )


def stacked_query(q_ref, kv_head):
    heads = range(kv_head * G, (kv_head + 1) * G)
    return jnp.concatenate([q_ref[0, :, h * HD : (h + 1) * HD] for h in heads], axis=0)


def masked_scores(query, key_ref, kv_head, bound):
    keys = key_ref[0, :, kv_head * HD : (kv_head + 1) * HD]
    scores = lax.dot_general(query, keys, (((1,), (1,)), ((), ())), preferred_element_type=jnp.float32)
    stacked, length = scores.shape
    row = lax.rem(lax.broadcasted_iota(jnp.int32, (stacked, 1), 0), jnp.int32(stacked // G))
    visible = lax.broadcasted_iota(jnp.int32, (1, length), 1) <= row + bound
    return jnp.where(visible, scores, NEG_FILL)


def attend(query, key_refs, value_refs, kv_head, bounds):
    columns = slice(kv_head * HD, (kv_head + 1) * HD)
    parts = [masked_scores(query, ref, kv_head, bound) for ref, bound in zip(key_refs, bounds)]
    top = functools.reduce(jnp.maximum, [jnp.max(part, axis=1, keepdims=True) for part in parts])
    top = jnp.maximum(top, MAX_FLOOR)
    weights = [jnp.exp2((part - top) * EXP_SCALE) for part in parts]
    total = sum(jnp.sum(part, axis=1, keepdims=True) for part in weights)
    mixed = sum(
        jnp.dot(part.astype(jnp.bfloat16), ref[0, :, columns], preferred_element_type=jnp.float32)
        for part, ref in zip(weights, value_refs)
    )
    some = total > 0.0
    total = jnp.where(some, total, 1.0)
    return mixed / total, jnp.where(some, top * EXP_SCALE + jnp.log(total) * LOG2_E, NEG_FILL)


def copy_all(pairs, sems):
    copies = [pltpu.make_async_copy(source, target, sems.at[i]) for i, (source, target) in enumerate(pairs)]
    for copy in copies:
        copy.start()
    return copies


def query_kernel(q_hbm, *refs):
    *query_refs, sems = refs
    rows = q_hbm.shape[1]
    heads = [(query_ref, g) for query_ref in query_refs for g in range(G)]
    parts = [(q_hbm.at[0, :, pl.ds(h * HD, HD)], ref.at[pl.ds(g * rows, rows)]) for h, (ref, g) in enumerate(heads)]
    for copy in copy_all(parts, sems):
        copy.wait()


def cache_kernel(key_hbm, value_hbm, w_hbm, key_ref, value_ref, w_ref, sems):
    span = pl.ds(0, w_ref.shape[1])
    for copy in copy_all(((key_hbm, key_ref), (value_hbm, value_ref), (w_hbm.at[:, span], w_ref)), sems):
        copy.wait()


def bounds_of(masks, offset, block, rows, length):
    own = lax.axis_index("ctx")
    return [offset + block * rows - (own ^ mask) * length for mask in masks]


def near_kernel(masks, kv_local, offset_ref, w_hbm, *refs):
    count = len(masks)
    query_refs, refs = refs[:kv_local], refs[kv_local:]
    key_refs, value_refs, refs = refs[:count], refs[count : 2 * count], refs[2 * count :]
    result_ref, log_ref, *w_refs, sems = refs
    heights = [ref.shape[1] for ref in w_refs]
    parts = [w_hbm.at[:, pl.ds((i + 1) * height, height)] for i, height in enumerate(heights)]
    copies = copy_all(zip(parts, w_refs), sems)
    rows, length = query_refs[0].shape[0] // G, key_refs[0].shape[1]
    bounds = bounds_of(masks, offset_ref[0], lax.axis_index("ctx"), rows, length)
    for kv_head, query_ref in enumerate(query_refs):
        result, log_sum = attend(query_ref[...], key_refs, value_refs, kv_head, bounds)
        result_ref[kv_head] = result
        log_ref[kv_head] = jnp.broadcast_to(log_sum, log_ref.shape[1:])
    for copy in copies:
        copy.wait()


def far_kernel(masks, far, kv_head, offset_ref, query_ref, *refs):
    count = len(masks)
    key_refs, value_refs, (out_ref,) = refs[:count], refs[count : 2 * count], refs[2 * count :]
    stacked = query_ref.shape[0]
    rows, length = stacked // G, key_refs[0].shape[1]
    bounds = bounds_of(masks, offset_ref[0], lax.axis_index("ctx") ^ far, rows, length)
    result, log_sum = attend(query_ref[...], key_refs, value_refs, kv_head, bounds)
    out_ref[:stacked] = result.astype(jnp.bfloat16)
    lane = lax.broadcasted_iota(jnp.int32, (rows, LANES), 1)
    logs = jnp.zeros((rows, LANES), jnp.float32)
    for g in range(G):
        logs = jnp.where(lane == g, log_sum[g * rows : (g + 1) * rows], logs)
    logs = logs.T[:LOG_ROWS]
    high = logs.astype(jnp.bfloat16).astype(jnp.float32)
    middle = (logs - high).astype(jnp.bfloat16).astype(jnp.float32)
    low = logs - high - middle
    rest = jnp.zeros((LOG_SPACE - 3 * LOG_ROWS, rows), jnp.float32)
    out_ref[stacked:] = jnp.concatenate([high, middle, low, rest], axis=0).astype(jnp.bfloat16)


def block_columns(group, slot, block_width):
    xs, lower, width = group
    return pl.ds(pl.multiple_of((lax.axis_index("tp") ^ xs[slot]) * block_width + lower, LANES), width)


def projected_block(att_refs, w_refs, columns):
    return sum(
        jnp.dot(att_ref[...], w_ref[0, :, columns], preferred_element_type=jnp.float32)
        for att_ref, w_ref in zip(att_refs, w_refs)
    )


def combine_kernel(kv_head, group, block_width, near_ref, log_ref, far_ref, w_ref, *refs):
    *before_refs, att_ref, send_ref = refs
    rows = att_ref.shape[0]
    stacked = G * rows
    parts = far_ref[stacked:].astype(jnp.float32)
    logs = sum(parts[i * LOG_ROWS : (i + 1) * LOG_ROWS] for i in range(3))
    logs = jnp.concatenate([logs, jnp.zeros((LANES - LOG_ROWS, rows), jnp.float32)], axis=0).T
    for g in range(G):
        span = slice(g * rows, (g + 1) * rows)
        near_log, far_log = log_ref[kv_head, span, :1], logs[:, g : g + 1]
        top = jnp.maximum(near_log, far_log)
        near_weight, far_weight = jnp.exp2(near_log - top), jnp.exp2(far_log - top)
        scale = 1.0 / (near_weight + far_weight)
        mixed = near_ref[kv_head, span] * (near_weight * scale)
        mixed += far_ref[span].astype(jnp.float32) * (far_weight * scale)
        att_ref[:, g * HD : (g + 1) * HD] = mixed.astype(jnp.bfloat16)
    for slot in range(len(group[0])):
        block = projected_block([att_ref], [w_ref], block_columns(group, slot, block_width))
        for before_ref in before_refs:
            block += before_ref[slot]
        send_ref[slot] = block.astype(send_ref.dtype)


def own_kernel(count, group, block_width, *refs):
    att_refs, w_refs, (residual_ref, own_ref) = refs[:count], refs[count : 2 * count], refs[2 * count :]
    own = projected_block(att_refs, w_refs, block_columns(group, 0, block_width))
    own_ref[...] = (residual_ref[0, :, : own_ref.shape[1]].astype(jnp.float32) + own).astype(jnp.bfloat16)


def project_kernel(count, groups, block_width, *refs):
    att_refs, w_refs, out_refs = refs[:count], refs[count : 2 * count], refs[2 * count :]
    for group, out_ref in zip(groups, out_refs):
        for slot in range(len(group[0])):
            block = projected_block(att_refs, w_refs, block_columns(group, slot, block_width))
            out_ref[slot] = block.astype(jnp.bfloat16)


def total_kernel(count, *refs):
    *term_refs, out_ref, total_ref, sems = refs
    lower = term_refs[0].shape[1]
    half = out_ref.shape[0] // 2
    copies = []
    for i, rows in enumerate((slice(0, half), slice(half, 2 * half))):
        for group, columns in ((term_refs[:count], slice(0, lower)), (term_refs[count:], slice(lower, None))):
            total_ref[rows, columns] = sum(ref[rows].astype(jnp.float32) for ref in group).astype(jnp.bfloat16)
        copies.append(pltpu.make_async_copy(total_ref.at[rows], out_ref.at[rows], sems.at[i]))
        copies[-1].start()
    for copy in copies:
        copy.wait()


def xor_order(lowest, size):
    if lowest >= size:
        return [0]
    rest = xor_order(lowest * 2, size)
    return [x + lowest for x in rest] + rest


def cross_first_width(width):
    return max(1, (3 * (width // LANES)) // 10) * LANES


def on_device(row_offsets, queries, cache_keys, cache_values, residual, out_weight):
    n_ctx, n_tp = lax.axis_size("ctx"), lax.axis_size("tp")
    rows = queries.shape[1]
    kv_local = cache_keys.shape[2] // HD
    stacked = G * rows
    top_bit = n_ctx // 2
    block_width = out_weight.shape[2] // n_tp
    bf16, f32 = jnp.bfloat16, jnp.float32

    in_hbm = [pltpu.with_memory_space_constraint(a, pltpu.HBM) for a in (queries, cache_keys, cache_values, out_weight)]
    own_queries = local_call(
        query_kernel,
        [IN_HBM],
        [((stacked, HD), bf16)] * kv_local,
        16 * MIB,
        0,
        [pltpu.SemaphoreType.DMA((kv_local * G,))],
    )(in_hbm[0])
    near = [(0, cache_keys, cache_values)]
    bit = top_bit // 2
    while bit:
        near += [(m | bit, exchange(k, "ctx", bit), exchange(v, "ctx", bit)) for m, k, v in near]
        bit //= 2
    w_shape = (1, G * HD, out_weight.shape[2])
    own_keys, own_values, first_weight = local_call(
        cache_kernel,
        [IN_HBM] * 3,
        [(cache_keys.shape, bf16), (cache_values.shape, bf16), (w_shape, bf16)],
        16 * MIB,
        0,
        [pltpu.SemaphoreType.DMA((3,))],
    )(*in_hbm[1:])
    sent_queries = list(own_queries)
    sent_queries[1:], first_weight = lax.optimization_barrier((sent_queries[1:], first_weight))
    far_queries = [exchange(query, "ctx", top_bit) for query in sent_queries]
    masks, near_keys, near_values = zip(*near)
    cached = [in_vmem(a) for a in (own_keys, *near_keys[1:], own_values, *near_values[1:])]
    far_results = []
    for kv_head in range(kv_local):
        query = far_queries[kv_head]
        if kv_head:
            query, _ = lax.optimization_barrier((query, result))
        (result,) = local_call(
            functools.partial(far_kernel, masks, top_bit, kv_head),
            [SCALARS] + [WHOLE] * (1 + len(cached)),
            [((stacked + LOG_SPACE, HD), bf16)],
            24 * MIB,
            0,
        )(row_offsets, in_vmem(query), *cached)
        far_results.append(exchange(result, "ctx", top_bit))
    near_result, near_log, *weights = local_call(
        functools.partial(near_kernel, masks, kv_local),
        [SCALARS, IN_HBM] + [WHOLE] * (kv_local + len(cached)),
        [((kv_local, stacked, HD), f32)] * 2 + [(w_shape, bf16)] * (kv_local - 1),
        24 * MIB,
        0,
        [pltpu.SemaphoreType.DMA((kv_local,))],
    )(row_offsets, in_hbm[3], *own_queries, *cached)
    weights = [first_weight, *weights]

    across = xor_order(2, n_tp)[:-1]
    cross_width = cross_first_width(block_width)
    pair_width = block_width - cross_width
    block_flops = 2 * rows * out_weight.shape[1]
    relay = ([1 ^ x for x in across], 0, pair_width)
    attended, sent = [], []
    for kv_head, result in enumerate(far_results):
        kind = bf16 if kv_head + 1 == kv_local else f32
        head, *sent = local_call(
            functools.partial(combine_kernel, kv_head, relay, block_width),
            [WHOLE] * (4 + len(sent)),
            [((rows, G * HD), bf16), ((len(across), rows, pair_width), kind)],
            24 * MIB,
            0,
        )(near_result, near_log, in_vmem(result), weights[kv_head], *sent)
        attended.append(head)
    (send_a,) = sent
    (own_a,) = local_call(
        functools.partial(own_kernel, kv_local, ([0], 0, pair_width), block_width),
        [WHOLE] * (2 * kv_local + 1),
        [((rows, pair_width), bf16)],
        16 * MIB,
        block_flops * pair_width,
    )(*attended, *weights, in_vmem(residual))

    def projected(*groups):
        return local_call(
            functools.partial(project_kernel, kv_local, groups, block_width),
            [WHOLE] * (2 * kv_local),
            [((len(xs), rows, width), bf16) for xs, _, width in groups],
            16 * MIB,
            block_flops * sum(len(xs) * width for xs, _, width in groups),
        )(*attended, *weights)

    half = n_tp // 2
    own_a = handed(own_a, 0)
    send_b, pair_a = projected((list(range(half, n_tp)), pair_width, cross_width), ([1], 0, pair_width))
    kept_a, kept_b = projected((across, 0, pair_width), (list(range(half)), pair_width, cross_width))
    got_a = exchange(send_a, "tp", 1)
    got_b = exchange(send_b, "tp", half)
    pair_a = handed(pair_a[0], 1)

    part = [kept_a[i].astype(jnp.float32) + got_a[i].astype(jnp.float32) for i in range(len(across))]
    own_a, *part = lax.optimization_barrier((own_a, *[a.astype(jnp.bfloat16) for a in part]))
    terms_a = [own_a, pair_a]
    bit = 2
    while bit < n_tp:
        count = (len(part) + 1) // 2
        sends = part[:count]
        received = [exchange(a, "tp", bit) for a in sends[:-1]]
        terms_a.append(handed(sends[-1], bit))
        part = [(a.astype(jnp.float32) + r.astype(jnp.float32)).astype(jnp.bfloat16) for a, r in zip(part[count:], received)]
        bit *= 2

    part = [kept_b[i].astype(jnp.float32) + got_b[i].astype(jnp.float32) for i in range(half)]
    while len(part) > 2:
        count = len(part) // 2
        received = [exchange(a.astype(jnp.bfloat16), "tp", count) for a in part[count:]]
        part = [a + r.astype(jnp.float32) for a, r in zip(part[:count], received)]
    part[0] = part[0] + residual[0, :, pair_width:].astype(jnp.float32)
    part = [a.astype(jnp.bfloat16) for a in part]
    terms_b = [handed(a, x) for x, a in enumerate(part)]

    terms = [*terms_a, *terms_b]
    (out,) = pl.pallas_call(
        functools.partial(total_kernel, len(terms_a)),
        in_specs=[WHOLE] * len(terms),
        out_shape=[pltpu.HBM((rows, block_width), jnp.bfloat16)],
        out_specs=[IN_HBM],
        scratch_shapes=[pltpu.VMEM((rows, block_width), jnp.bfloat16), pltpu.SemaphoreType.DMA((2,))],
        compiler_params=pltpu.CompilerParams(vmem_limit_bytes=16 * MIB),
    )(*[in_vmem(term) for term in terms])
    return out[None]


def solution(mesh):
    placed = (
        P("section"),
        P("section", "ctx", "tp"),
        P("section", "ctx", "tp"),
        P("section", "ctx", "tp"),
        P("section", "ctx", "tp"),
        P("section", "tp", None),
    )
    return jax.shard_map(
        on_device, mesh=mesh, in_specs=placed, out_specs=P("section", "ctx", "tp"), check_vma=False
    )
```

```python
import functools
import math

import jax
import jax.numpy as jnp
from jax import lax
from jax.experimental import pallas as pl
from jax.experimental.pallas import tpu as pltpu
from jax.sharding import PartitionSpec as P

HD = 128
G = 4
LANES = 128
NEG_FILL = -1e30
MAX_FLOOR = -1e29
EXP_SCALE = HD ** (-0.5) * math.log2(math.e)
LOG2_E = math.log2(math.e)
LOG_ROWS = G
LOG_SPACE = 16
MIB = 1 << 20

WHOLE = pl.BlockSpec(memory_space=pltpu.VMEM)
IN_HBM = pl.BlockSpec(memory_space=pltpu.HBM)
SCALARS = pl.BlockSpec(memory_space=pltpu.SMEM)


def exchange(block, axis, mask):
    route = [(i, i ^ mask) for i in range(lax.axis_size(axis))]
    return lax.ppermute(block, axis, route)


def handed(block, mask):
    sections, n_tp = lax.axis_size("section"), lax.axis_size("tp")
    route = [(s * n_tp + i, (s + 1) % sections * n_tp + (i ^ mask)) for s in range(sections) for i in range(n_tp)]
    return lax.ppermute(block, ("section", "tp"), route)


def in_vmem(array):
    return pltpu.with_memory_space_constraint(array, pltpu.VMEM)


def local_call(body, ins, outs, limit, flops, scratch=()):
    return pl.pallas_call(
        body,
        in_specs=ins,
        out_shape=[pltpu.VMEM(shape, dtype) for shape, dtype in outs],
        out_specs=[WHOLE] * len(outs),
        scratch_shapes=list(scratch),
        compiler_params=pltpu.CompilerParams(vmem_limit_bytes=limit),
        cost_estimate=pl.CostEstimate(flops=flops, bytes_accessed=0, transcendentals=0),
    )


def masked_scores(query, key_ref, kv_head, bound):
    keys = key_ref[0, :, kv_head * HD : (kv_head + 1) * HD]
    scores = lax.dot_general(query, keys, (((1,), (1,)), ((), ())), preferred_element_type=jnp.float32)
    stacked, length = scores.shape
    row = lax.rem(lax.broadcasted_iota(jnp.int32, (stacked, 1), 0), jnp.int32(stacked // G))
    visible = lax.broadcasted_iota(jnp.int32, (1, length), 1) <= row + bound
    return jnp.where(visible, scores, NEG_FILL)


def attend(query, key_refs, value_refs, kv_head, bounds):
    columns = slice(kv_head * HD, (kv_head + 1) * HD)
    parts = [masked_scores(query, ref, kv_head, bound) for ref, bound in zip(key_refs, bounds)]
    top = functools.reduce(jnp.maximum, [jnp.max(part, axis=1, keepdims=True) for part in parts])
    top = jnp.maximum(top, MAX_FLOOR)
    weights = [jnp.exp2((part - top) * EXP_SCALE) for part in parts]
    total = sum(jnp.sum(part, axis=1, keepdims=True) for part in weights)
    mixed = sum(
        jnp.dot(part.astype(jnp.bfloat16), ref[0, :, columns], preferred_element_type=jnp.float32)
        for part, ref in zip(weights, value_refs)
    )
    some = total > 0.0
    total = jnp.where(some, total, 1.0)
    return mixed / total, jnp.where(some, top * EXP_SCALE + jnp.log(total) * LOG2_E, NEG_FILL)


def copy_all(pairs, sems):
    copies = [pltpu.make_async_copy(source, target, sems.at[i]) for i, (source, target) in enumerate(pairs)]
    for copy in copies:
        copy.start()
    return copies


def query_kernel(q_hbm, *refs):
    *query_refs, sems = refs
    rows = q_hbm.shape[1]
    heads = [(query_ref, g) for query_ref in query_refs for g in range(G)]
    parts = [(q_hbm.at[0, :, pl.ds(h * HD, HD)], ref.at[pl.ds(g * rows, rows)]) for h, (ref, g) in enumerate(heads)]
    for copy in copy_all(parts, sems):
        copy.wait()


def cache_kernel(key_hbm, value_hbm, w_hbm, key_ref, value_ref, w_ref, sems):
    span = pl.ds(0, w_ref.shape[1])
    for copy in copy_all(((key_hbm, key_ref), (value_hbm, value_ref), (w_hbm.at[:, span], w_ref)), sems):
        copy.wait()


def bounds_of(masks, offset, block, rows, length):
    own = lax.axis_index("ctx")
    return [offset + block * rows - (own ^ mask) * length for mask in masks]


def near_kernel(masks, kv_local, offset_ref, w_hbm, *refs):
    count = len(masks)
    query_refs, refs = refs[:kv_local], refs[kv_local:]
    key_refs, value_refs, refs = refs[:count], refs[count : 2 * count], refs[2 * count :]
    result_ref, log_ref, *w_refs, sems = refs
    heights = [ref.shape[1] for ref in w_refs]
    parts = [w_hbm.at[:, pl.ds((i + 1) * height, height)] for i, height in enumerate(heights)]
    copies = copy_all(zip(parts, w_refs), sems)
    rows, length = query_refs[0].shape[0] // G, key_refs[0].shape[1]
    bounds = bounds_of(masks, offset_ref[0], lax.axis_index("ctx"), rows, length)
    for kv_head, query_ref in enumerate(query_refs):
        result, log_sum = attend(query_ref[...], key_refs, value_refs, kv_head, bounds)
        result_ref[kv_head] = result
        log_ref[kv_head] = jnp.broadcast_to(log_sum, log_ref.shape[1:])
    for copy in copies:
        copy.wait()


def far_kernel(masks, far, kv_head, offset_ref, query_ref, *refs):
    count = len(masks)
    key_refs, value_refs, (out_ref,) = refs[:count], refs[count : 2 * count], refs[2 * count :]
    stacked = query_ref.shape[0]
    rows, length = stacked // G, key_refs[0].shape[1]
    bounds = bounds_of(masks, offset_ref[0], lax.axis_index("ctx") ^ far, rows, length)
    result, log_sum = attend(query_ref[...], key_refs, value_refs, kv_head, bounds)
    out_ref[:stacked] = result.astype(jnp.bfloat16)
    lane = lax.broadcasted_iota(jnp.int32, (rows, LANES), 1)
    logs = jnp.zeros((rows, LANES), jnp.float32)
    for g in range(G):
        logs = jnp.where(lane == g, log_sum[g * rows : (g + 1) * rows], logs)
    logs = logs.T[:LOG_ROWS]
    high = logs.astype(jnp.bfloat16).astype(jnp.float32)
    middle = (logs - high).astype(jnp.bfloat16).astype(jnp.float32)
    low = logs - high - middle
    rest = jnp.zeros((LOG_SPACE - 3 * LOG_ROWS, rows), jnp.float32)
    out_ref[stacked:] = jnp.concatenate([high, middle, low, rest], axis=0).astype(jnp.bfloat16)


def block_columns(group, slot, block_width):
    xs, lower, width = group
    return pl.ds(pl.multiple_of((lax.axis_index("tp") ^ xs[slot]) * block_width + lower, LANES), width)


def projected_block(att_refs, w_refs, columns):
    return sum(
        jnp.dot(att_ref[...], w_ref[0, :, columns], preferred_element_type=jnp.float32)
        for att_ref, w_ref in zip(att_refs, w_refs)
    )


def combine_kernel(kv_head, group, block_width, near_ref, log_ref, far_ref, w_ref, *refs):
    *before_refs, att_ref, send_ref = refs
    rows = att_ref.shape[0]
    stacked = G * rows
    parts = far_ref[stacked:].astype(jnp.float32)
    logs = sum(parts[i * LOG_ROWS : (i + 1) * LOG_ROWS] for i in range(3))
    logs = jnp.concatenate([logs, jnp.zeros((LANES - LOG_ROWS, rows), jnp.float32)], axis=0).T
    for g in range(G):
        span = slice(g * rows, (g + 1) * rows)
        near_log, far_log = log_ref[kv_head, span, :1], logs[:, g : g + 1]
        top = jnp.maximum(near_log, far_log)
        near_weight, far_weight = jnp.exp2(near_log - top), jnp.exp2(far_log - top)
        scale = 1.0 / (near_weight + far_weight)
        mixed = near_ref[kv_head, span] * (near_weight * scale)
        mixed += far_ref[span].astype(jnp.float32) * (far_weight * scale)
        att_ref[:, g * HD : (g + 1) * HD] = mixed.astype(jnp.bfloat16)
    for slot in range(len(group[0])):
        block = projected_block([att_ref], [w_ref], block_columns(group, slot, block_width))
        for before_ref in before_refs:
            block += before_ref[slot]
        send_ref[slot] = block.astype(send_ref.dtype)


def own_kernel(count, group, block_width, *refs):
    att_refs, w_refs, (residual_ref, own_ref) = refs[:count], refs[count : 2 * count], refs[2 * count :]
    own = projected_block(att_refs, w_refs, block_columns(group, 0, block_width))
    own_ref[...] = (residual_ref[0, :, : own_ref.shape[1]].astype(jnp.float32) + own).astype(jnp.bfloat16)


def project_kernel(count, groups, block_width, *refs):
    att_refs, w_refs, out_refs = refs[:count], refs[count : 2 * count], refs[2 * count :]
    for group, out_ref in zip(groups, out_refs):
        for slot in range(len(group[0])):
            block = projected_block(att_refs, w_refs, block_columns(group, slot, block_width))
            out_ref[slot] = block.astype(jnp.bfloat16)


def total_kernel(count, *refs):
    *term_refs, out_ref, total_ref, sems = refs
    lower = term_refs[0].shape[1]
    half = out_ref.shape[0] // 2
    copies = []
    for i, rows in enumerate((slice(0, half), slice(half, 2 * half))):
        for group, columns in ((term_refs[:count], slice(0, lower)), (term_refs[count:], slice(lower, None))):
            total_ref[rows, columns] = sum(ref[rows].astype(jnp.float32) for ref in group).astype(jnp.bfloat16)
        copies.append(pltpu.make_async_copy(total_ref.at[rows], out_ref.at[rows], sems.at[i]))
        copies[-1].start()
    for copy in copies:
        copy.wait()


def xor_order(lowest, size):
    if lowest >= size:
        return [0]
    rest = xor_order(lowest * 2, size)
    return [x + lowest for x in rest] + rest


def cross_first_width(width):
    return max(1, (3 * (width // LANES)) // 10) * LANES


def on_device(row_offsets, queries, cache_keys, cache_values, residual, out_weight):
    n_ctx, n_tp = lax.axis_size("ctx"), lax.axis_size("tp")
    rows = queries.shape[1]
    kv_local = cache_keys.shape[2] // HD
    stacked = G * rows
    top_bit = n_ctx // 2
    block_width = out_weight.shape[2] // n_tp
    bf16, f32 = jnp.bfloat16, jnp.float32

    in_hbm = [pltpu.with_memory_space_constraint(a, pltpu.HBM) for a in (queries, cache_keys, cache_values, out_weight)]
    own_queries = local_call(
        query_kernel,
        [IN_HBM],
        [((stacked, HD), bf16)] * kv_local,
        16 * MIB,
        0,
        [pltpu.SemaphoreType.DMA((kv_local * G,))],
    )(in_hbm[0])
    near = [(0, cache_keys, cache_values)]
    bit = top_bit // 2
    while bit:
        near += [(m | bit, exchange(k, "ctx", bit), exchange(v, "ctx", bit)) for m, k, v in near]
        bit //= 2
    w_shape = (1, G * HD, out_weight.shape[2])
    own_keys, own_values, first_weight = local_call(
        cache_kernel,
        [IN_HBM] * 3,
        [(cache_keys.shape, bf16), (cache_values.shape, bf16), (w_shape, bf16)],
        16 * MIB,
        0,
        [pltpu.SemaphoreType.DMA((3,))],
    )(*in_hbm[1:])
    sent_queries = list(own_queries)
    sent_queries[1:], first_weight = lax.optimization_barrier((sent_queries[1:], first_weight))
    far_queries = [exchange(query, "ctx", top_bit) for query in sent_queries]
    masks, near_keys, near_values = zip(*near)
    cached = [in_vmem(a) for a in (own_keys, *near_keys[1:], own_values, *near_values[1:])]
    far_results = []
    for kv_head in range(kv_local):
        query = far_queries[kv_head]
        if kv_head:
            query, _ = lax.optimization_barrier((query, result))
        (result,) = local_call(
            functools.partial(far_kernel, masks, top_bit, kv_head),
            [SCALARS] + [WHOLE] * (1 + len(cached)),
            [((stacked + LOG_SPACE, HD), bf16)],
            24 * MIB,
            0,
        )(row_offsets, in_vmem(query), *cached)
        far_results.append(exchange(result, "ctx", top_bit))
    near_result, near_log, *weights = local_call(
        functools.partial(near_kernel, masks, kv_local),
        [SCALARS, IN_HBM] + [WHOLE] * (kv_local + len(cached)),
        [((kv_local, stacked, HD), f32)] * 2 + [(w_shape, bf16)] * (kv_local - 1),
        24 * MIB,
        0,
        [pltpu.SemaphoreType.DMA((kv_local,))],
    )(row_offsets, in_hbm[3], *own_queries, *cached)
    weights = [first_weight, *weights]

    across = xor_order(2, n_tp)[:-1]
    cross_width = cross_first_width(block_width)
    pair_width = block_width - cross_width
    block_flops = 2 * rows * out_weight.shape[1]
    relay = ([1 ^ x for x in across], 0, pair_width)
    attended, sent = [], []
    for kv_head, result in enumerate(far_results):
        kind = bf16 if kv_head + 1 == kv_local else f32
        head, *sent = local_call(
            functools.partial(combine_kernel, kv_head, relay, block_width),
            [WHOLE] * (4 + len(sent)),
            [((rows, G * HD), bf16), ((len(across), rows, pair_width), kind)],
            24 * MIB,
            0,
        )(near_result, near_log, in_vmem(result), weights[kv_head], *sent)
        attended.append(head)
    (send_a,) = sent
    (own_a,) = local_call(
        functools.partial(own_kernel, kv_local, ([0], 0, pair_width), block_width),
        [WHOLE] * (2 * kv_local + 1),
        [((rows, pair_width), bf16)],
        16 * MIB,
        block_flops * pair_width,
    )(*attended, *weights, in_vmem(residual))

    def projected(*groups):
        return local_call(
            functools.partial(project_kernel, kv_local, groups, block_width),
            [WHOLE] * (2 * kv_local),
            [((len(xs), rows, width), bf16) for xs, _, width in groups],
            16 * MIB,
            block_flops * sum(len(xs) * width for xs, _, width in groups),
        )(*attended, *weights)

    half = n_tp // 2
    own_a = handed(own_a, 0)
    send_b, pair_a = projected((list(range(half, n_tp)), pair_width, cross_width), ([1], 0, pair_width))
    kept_a, kept_b = projected((across, 0, pair_width), (list(range(half)), pair_width, cross_width))
    got_a = exchange(send_a, "tp", 1)
    got_b = exchange(send_b, "tp", half)
    pair_a = handed(pair_a[0], 1)

    part = [kept_a[i].astype(jnp.float32) + got_a[i].astype(jnp.float32) for i in range(len(across))]
    own_a, *part = lax.optimization_barrier((own_a, *[a.astype(jnp.bfloat16) for a in part]))
    terms_a = [own_a, pair_a]
    bit = 2
    while bit < n_tp:
        count = (len(part) + 1) // 2
        sends = part[:count]
        received = [exchange(a, "tp", bit) for a in sends[:-1]]
        terms_a.append(handed(sends[-1], bit))
        part = [(a.astype(jnp.float32) + r.astype(jnp.float32)).astype(jnp.bfloat16) for a, r in zip(part[count:], received)]
        bit *= 2

    part = [kept_b[i].astype(jnp.float32) + got_b[i].astype(jnp.float32) for i in range(half)]
    while len(part) > 2:
        count = len(part) // 2
        received = [exchange(a.astype(jnp.bfloat16), "tp", count) for a in part[count:]]
        part = [a + r.astype(jnp.float32) for a, r in zip(part[:count], received)]
    part[0] = part[0] + residual[0, :, pair_width:].astype(jnp.float32)
    part = [a.astype(jnp.bfloat16) for a in part]
    terms_b = [handed(a, x) for x, a in enumerate(part)]

    terms = [*terms_a, *terms_b]
    (out,) = pl.pallas_call(
        functools.partial(total_kernel, len(terms_a)),
        in_specs=[WHOLE] * len(terms),
        out_shape=[pltpu.HBM((rows, block_width), jnp.bfloat16)],
        out_specs=[IN_HBM],
        scratch_shapes=[pltpu.VMEM((rows, block_width), jnp.bfloat16), pltpu.SemaphoreType.DMA((2,))],
        compiler_params=pltpu.CompilerParams(vmem_limit_bytes=16 * MIB),
    )(*[in_vmem(term) for term in terms])
    return out[None]


def solution(mesh):
    placed = (
        P("section"),
        P("section", "ctx", "tp"),
        P("section", "ctx", "tp"),
        P("section", "ctx", "tp"),
        P("section", "ctx", "tp"),
        P("section", "tp", None),
    )
    return jax.shard_map(
        on_device, mesh=mesh, in_specs=placed, out_specs=P("section", "ctx", "tp"), check_vma=False
    )
```

```python
import functools
import math

import jax
import jax.numpy as jnp
from jax import lax
from jax.experimental import pallas as pl
from jax.experimental.pallas import tpu as pltpu
from jax.sharding import PartitionSpec as P

HD = 128
G = 4
LANES = 128
NEG_FILL = -1e30
MAX_FLOOR = -1e29
EXP_SCALE = HD ** (-0.5) * math.log2(math.e)
LOG2_E = math.log2(math.e)
LOG_ROWS = G
LOG_SPACE = 16
MIB = 1 << 20

WHOLE = pl.BlockSpec(memory_space=pltpu.VMEM)
IN_HBM = pl.BlockSpec(memory_space=pltpu.HBM)
SCALARS = pl.BlockSpec(memory_space=pltpu.SMEM)


def exchange(block, axis, mask):
    route = [(i, i ^ mask) for i in range(lax.axis_size(axis))]
    return lax.ppermute(block, axis, route)


def handed(block, mask):
    sections, n_tp = lax.axis_size("section"), lax.axis_size("tp")
    route = [(s * n_tp + i, (s + 1) % sections * n_tp + (i ^ mask)) for s in range(sections) for i in range(n_tp)]
    return lax.ppermute(block, ("section", "tp"), route)


def in_vmem(array):
    return pltpu.with_memory_space_constraint(array, pltpu.VMEM)


def local_call(body, ins, outs, limit, flops, scratch=()):
    return pl.pallas_call(
        body,
        in_specs=ins,
        out_shape=[pltpu.VMEM(shape, dtype) for shape, dtype in outs],
        out_specs=[WHOLE] * len(outs),
        scratch_shapes=list(scratch),
        compiler_params=pltpu.CompilerParams(vmem_limit_bytes=limit),
        cost_estimate=pl.CostEstimate(flops=flops, bytes_accessed=0, transcendentals=0),
    )


def masked_scores(query, key_ref, kv_head, bound):
    keys = key_ref[0, :, kv_head * HD : (kv_head + 1) * HD]
    scores = lax.dot_general(query, keys, (((1,), (1,)), ((), ())), preferred_element_type=jnp.float32)
    stacked, length = scores.shape
    row = lax.rem(lax.broadcasted_iota(jnp.int32, (stacked, 1), 0), jnp.int32(stacked // G))
    visible = lax.broadcasted_iota(jnp.int32, (1, length), 1) <= row + bound
    return jnp.where(visible, scores, NEG_FILL)


def attend(query, key_refs, value_refs, kv_head, bounds):
    columns = slice(kv_head * HD, (kv_head + 1) * HD)
    parts = [masked_scores(query, ref, kv_head, bound) for ref, bound in zip(key_refs, bounds)]
    top = functools.reduce(jnp.maximum, [jnp.max(part, axis=1, keepdims=True) for part in parts])
    top = jnp.maximum(top, MAX_FLOOR)
    weights = [jnp.exp2((part - top) * EXP_SCALE) for part in parts]
    total = sum(jnp.sum(part, axis=1, keepdims=True) for part in weights)
    mixed = sum(
        jnp.dot(part.astype(jnp.bfloat16), ref[0, :, columns], preferred_element_type=jnp.float32)
        for part, ref in zip(weights, value_refs)
    )
    some = total > 0.0
    total = jnp.where(some, total, 1.0)
    return mixed / total, jnp.where(some, top * EXP_SCALE + jnp.log(total) * LOG2_E, NEG_FILL)


def copy_all(pairs, sems):
    copies = [pltpu.make_async_copy(source, target, sems.at[i]) for i, (source, target) in enumerate(pairs)]
    for copy in copies:
        copy.start()
    return copies


def stacking(q_hbm, head, query_refs):
    rows = q_hbm.shape[1]
    places = [(query_ref, g) for query_ref in query_refs for g in range(G)]
    return [
        (q_hbm.at[0, :, pl.ds((head + i) * HD, HD)], ref.at[pl.ds(g * rows, rows)]) for i, (ref, g) in enumerate(places)
    ]


def query_kernel(q_hbm, query_ref, sems):
    for copy in copy_all(stacking(q_hbm, 0, [query_ref]), sems):
        copy.wait()


def cache_kernel(q_hbm, key_hbm, value_hbm, w_hbm, *refs):
    *query_refs, key_ref, value_ref, w_ref, sems = refs
    pairs = stacking(q_hbm, G, query_refs) + [(key_hbm, key_ref), (value_hbm, value_ref)]
    for copy in copy_all(pairs + [(w_hbm.at[:, pl.ds(0, w_ref.shape[1])], w_ref)], sems):
        copy.wait()


def bounds_of(masks, offset, block, rows, length):
    own = lax.axis_index("ctx")
    return [offset + block * rows - (own ^ mask) * length for mask in masks]


def near_kernel(masks, kv_local, offset_ref, w_hbm, *refs):
    count = len(masks)
    query_refs, refs = refs[:kv_local], refs[kv_local:]
    key_refs, value_refs, refs = refs[:count], refs[count : 2 * count], refs[2 * count :]
    result_ref, log_ref, *w_refs, sems = refs
    heights = [ref.shape[1] for ref in w_refs]
    parts = [w_hbm.at[:, pl.ds((i + 1) * height, height)] for i, height in enumerate(heights)]
    copies = copy_all(zip(parts, w_refs), sems)
    rows, length = query_refs[0].shape[0] // G, key_refs[0].shape[1]
    bounds = bounds_of(masks, offset_ref[0], lax.axis_index("ctx"), rows, length)
    for kv_head, query_ref in enumerate(query_refs):
        result, log_sum = attend(query_ref[...], key_refs, value_refs, kv_head, bounds)
        result_ref[kv_head] = result
        log_ref[kv_head] = jnp.broadcast_to(log_sum, log_ref.shape[1:])
    for copy in copies:
        copy.wait()


def far_kernel(masks, far, kv_head, offset_ref, query_ref, *refs):
    count = len(masks)
    key_refs, value_refs, (out_ref,) = refs[:count], refs[count : 2 * count], refs[2 * count :]
    stacked = query_ref.shape[0]
    rows, length = stacked // G, key_refs[0].shape[1]
    bounds = bounds_of(masks, offset_ref[0], lax.axis_index("ctx") ^ far, rows, length)
    result, log_sum = attend(query_ref[...], key_refs, value_refs, kv_head, bounds)
    out_ref[:stacked] = result.astype(jnp.bfloat16)
    lane = lax.broadcasted_iota(jnp.int32, (rows, LANES), 1)
    logs = jnp.zeros((rows, LANES), jnp.float32)
    for g in range(G):
        logs = jnp.where(lane == g, log_sum[g * rows : (g + 1) * rows], logs)
    logs = logs.T[:LOG_ROWS]
    high = logs.astype(jnp.bfloat16).astype(jnp.float32)
    middle = (logs - high).astype(jnp.bfloat16).astype(jnp.float32)
    low = logs - high - middle
    rest = jnp.zeros((LOG_SPACE - 3 * LOG_ROWS, rows), jnp.float32)
    out_ref[stacked:] = jnp.concatenate([high, middle, low, rest], axis=0).astype(jnp.bfloat16)


def block_columns(group, slot, block_width):
    xs, lower, width = group
    return pl.ds(pl.multiple_of((lax.axis_index("tp") ^ xs[slot]) * block_width + lower, LANES), width)


def projected_block(att_refs, w_refs, columns):
    return sum(
        jnp.dot(att_ref[...], w_ref[0, :, columns], preferred_element_type=jnp.float32)
        for att_ref, w_ref in zip(att_refs, w_refs)
    )


def combine_kernel(kv_head, group, block_width, near_ref, log_ref, far_ref, w_ref, *refs):
    *before_refs, att_ref, send_ref = refs
    rows = att_ref.shape[0]
    stacked = G * rows
    parts = far_ref[stacked:].astype(jnp.float32)
    logs = sum(parts[i * LOG_ROWS : (i + 1) * LOG_ROWS] for i in range(3))
    logs = jnp.concatenate([logs, jnp.zeros((LANES - LOG_ROWS, rows), jnp.float32)], axis=0).T
    for g in range(G):
        span = slice(g * rows, (g + 1) * rows)
        near_log, far_log = log_ref[kv_head, span, :1], logs[:, g : g + 1]
        top = jnp.maximum(near_log, far_log)
        near_weight, far_weight = jnp.exp2(near_log - top), jnp.exp2(far_log - top)
        scale = 1.0 / (near_weight + far_weight)
        mixed = near_ref[kv_head, span] * (near_weight * scale)
        mixed += far_ref[span].astype(jnp.float32) * (far_weight * scale)
        att_ref[:, g * HD : (g + 1) * HD] = mixed.astype(jnp.bfloat16)
    for slot in range(len(group[0])):
        block = projected_block([att_ref], [w_ref], block_columns(group, slot, block_width))
        for before_ref in before_refs:
            block += before_ref[slot]
        send_ref[slot] = block.astype(send_ref.dtype)


def own_kernel(count, group, block_width, *refs):
    att_refs, w_refs, (residual_ref, own_ref) = refs[:count], refs[count : 2 * count], refs[2 * count :]
    own = projected_block(att_refs, w_refs, block_columns(group, 0, block_width))
    own_ref[...] = (residual_ref[0, :, : own_ref.shape[1]].astype(jnp.float32) + own).astype(jnp.bfloat16)


def project_kernel(count, groups, block_width, *refs):
    att_refs, w_refs, out_refs = refs[:count], refs[count : 2 * count], refs[2 * count :]
    for group, out_ref in zip(groups, out_refs):
        for slot in range(len(group[0])):
            block = projected_block(att_refs, w_refs, block_columns(group, slot, block_width))
            out_ref[slot] = block.astype(jnp.bfloat16)


def total_kernel(count, *refs):
    *term_refs, out_ref, total_ref, sems = refs
    lower = term_refs[0].shape[1]
    part = out_ref.shape[0] // 4
    copies = []
    for i, rows in enumerate([slice(k * part, (k + 1) * part) for k in range(4)]):
        for group, columns in ((term_refs[:count], slice(0, lower)), (term_refs[count:], slice(lower, None))):
            total_ref[rows, columns] = sum(ref[rows].astype(jnp.float32) for ref in group).astype(jnp.bfloat16)
        copies.append(pltpu.make_async_copy(total_ref.at[rows], out_ref.at[rows], sems.at[i]))
        copies[-1].start()
    for copy in copies:
        copy.wait()


def xor_order(lowest, size):
    if lowest >= size:
        return [0]
    rest = xor_order(lowest * 2, size)
    return [x + lowest for x in rest] + rest


def cross_first_width(width):
    return max(1, (3 * (width // LANES)) // 10) * LANES


def on_device(row_offsets, queries, cache_keys, cache_values, residual, out_weight):
    n_ctx, n_tp = lax.axis_size("ctx"), lax.axis_size("tp")
    rows = queries.shape[1]
    kv_local = cache_keys.shape[2] // HD
    stacked = G * rows
    top_bit = n_ctx // 2
    block_width = out_weight.shape[2] // n_tp
    bf16, f32 = jnp.bfloat16, jnp.float32

    in_hbm = [pltpu.with_memory_space_constraint(a, pltpu.HBM) for a in (queries, cache_keys, cache_values, out_weight)]
    first_query = local_call(
        query_kernel, [IN_HBM], [((stacked, HD), bf16)], 16 * MIB, 0, [pltpu.SemaphoreType.DMA((G,))]
    )(in_hbm[0])
    near = [(0, cache_keys, cache_values)]
    bit = top_bit // 2
    while bit:
        near += [(m | bit, exchange(k, "ctx", bit), exchange(v, "ctx", bit)) for m, k, v in near]
        bit //= 2
    w_shape = (1, G * HD, out_weight.shape[2])
    *more_queries, own_keys, own_values, first_weight = local_call(
        cache_kernel,
        [IN_HBM] * 4,
        [((stacked, HD), bf16)] * (kv_local - 1)
        + [(cache_keys.shape, bf16), (cache_values.shape, bf16), (w_shape, bf16)],
        16 * MIB,
        0,
        [pltpu.SemaphoreType.DMA(((kv_local - 1) * G + 3,))],
    )(*in_hbm)
    own_queries = [*first_query, *more_queries]
    far_queries = [exchange(query, "ctx", top_bit) for query in own_queries]
    masks, near_keys, near_values = zip(*near)
    cached = [in_vmem(a) for a in (own_keys, *near_keys[1:], own_values, *near_values[1:])]
    far_results = []
    for kv_head in range(kv_local):
        query = far_queries[kv_head]
        if kv_head:
            query, _ = lax.optimization_barrier((query, result))
        (result,) = local_call(
            functools.partial(far_kernel, masks, top_bit, kv_head),
            [SCALARS] + [WHOLE] * (1 + len(cached)),
            [((stacked + LOG_SPACE, HD), bf16)],
            24 * MIB,
            0,
        )(row_offsets, in_vmem(query), *cached)
        far_results.append(exchange(result, "ctx", top_bit))
    near_result, near_log, *weights = local_call(
        functools.partial(near_kernel, masks, kv_local),
        [SCALARS, IN_HBM] + [WHOLE] * (kv_local + len(cached)),
        [((kv_local, stacked, HD), f32)] * 2 + [(w_shape, bf16)] * (kv_local - 1),
        24 * MIB,
        0,
        [pltpu.SemaphoreType.DMA((kv_local,))],
    )(row_offsets, in_hbm[3], *own_queries, *cached)
    weights = [first_weight, *weights]

    across = xor_order(2, n_tp)[:-1]
    cross_width = cross_first_width(block_width)
    pair_width = block_width - cross_width
    block_flops = 2 * rows * out_weight.shape[1]
    relay = ([1 ^ x for x in across], 0, pair_width)
    attended, sent = [], []
    for kv_head, result in enumerate(far_results):
        kind = bf16 if kv_head + 1 == kv_local else f32
        head, *sent = local_call(
            functools.partial(combine_kernel, kv_head, relay, block_width),
            [WHOLE] * (4 + len(sent)),
            [((rows, G * HD), bf16), ((len(across), rows, pair_width), kind)],
            24 * MIB,
            0,
        )(near_result, near_log, in_vmem(result), weights[kv_head], *sent)
        attended.append(head)
    (send_a,) = sent
    (own_a,) = local_call(
        functools.partial(own_kernel, kv_local, ([0], 0, pair_width), block_width),
        [WHOLE] * (2 * kv_local + 1),
        [((rows, pair_width), bf16)],
        16 * MIB,
        block_flops * pair_width,
    )(*attended, *weights, in_vmem(residual))

    def projected(*groups):
        return local_call(
            functools.partial(project_kernel, kv_local, groups, block_width),
            [WHOLE] * (2 * kv_local),
            [((len(xs), rows, width), bf16) for xs, _, width in groups],
            16 * MIB,
            block_flops * sum(len(xs) * width for xs, _, width in groups),
        )(*attended, *weights)

    half = n_tp // 2
    own_a = handed(own_a, 0)
    send_b, pair_a = projected((list(range(half, n_tp)), pair_width, cross_width), ([1], 0, pair_width))
    kept_a, kept_b = projected((across, 0, pair_width), (list(range(half)), pair_width, cross_width))
    got_a = exchange(send_a, "tp", 1)
    got_b = exchange(send_b, "tp", half)
    pair_a = handed(pair_a[0], 1)

    part = [kept_a[i].astype(jnp.float32) + got_a[i].astype(jnp.float32) for i in range(len(across))]
    own_a, *part = lax.optimization_barrier((own_a, *[a.astype(jnp.bfloat16) for a in part]))
    terms_a = [own_a, pair_a]
    bit = 2
    while bit < n_tp:
        count = (len(part) + 1) // 2
        sends = part[:count]
        received = [exchange(a, "tp", bit) for a in sends[:-1]]
        terms_a.append(handed(sends[-1], bit))
        part = [(a.astype(jnp.float32) + r.astype(jnp.float32)).astype(jnp.bfloat16) for a, r in zip(part[count:], received)]
        bit *= 2

    part = [kept_b[i].astype(jnp.float32) + got_b[i].astype(jnp.float32) for i in range(half)]
    while len(part) > 2:
        count = len(part) // 2
        received = [exchange(a.astype(jnp.bfloat16), "tp", count) for a in part[count:]]
        part = [a + r.astype(jnp.float32) for a, r in zip(part[:count], received)]
    part[0] = part[0] + residual[0, :, pair_width:].astype(jnp.float32)
    part = [a.astype(jnp.bfloat16) for a in part]
    terms_b = [handed(a, x) for x, a in enumerate(part)]

    terms_b, terms_a[-1] = lax.optimization_barrier((terms_b, terms_a[-1]))
    terms = [*terms_a, *terms_b]
    (out,) = pl.pallas_call(
        functools.partial(total_kernel, len(terms_a)),
        in_specs=[WHOLE] * len(terms),
        out_shape=[pltpu.HBM((rows, block_width), jnp.bfloat16)],
        out_specs=[IN_HBM],
        scratch_shapes=[pltpu.VMEM((rows, block_width), jnp.bfloat16), pltpu.SemaphoreType.DMA((4,))],
        compiler_params=pltpu.CompilerParams(vmem_limit_bytes=16 * MIB),
    )(*[in_vmem(term) for term in terms])
    return out[None]


def solution(mesh):
    placed = (
        P("section"),
        P("section", "ctx", "tp"),
        P("section", "ctx", "tp"),
        P("section", "ctx", "tp"),
        P("section", "ctx", "tp"),
        P("section", "tp", None),
    )
    return jax.shard_map(
        on_device, mesh=mesh, in_specs=placed, out_specs=P("section", "ctx", "tp"), check_vma=False
    )
```
